512 devices in a mesh: group: 32 (over z, core), row: 16 (over x, y).
Axes of the slice: x: 4, y: 4, z: 16, core: 2. Of those that a mesh axis runs over, the one named last changes fastest.
Arguments:
- queries: bfloat16 [64, 16, 64, 2560], P('group', 'row'), may hold values from -5 to 5
- keys: bfloat16 [64, 16, 64, 2560], P('group', 'row'), may hold values from -5 to 5
- values: bfloat16 [64, 16, 64, 2560], P('group', 'row'), may hold values from -6 to 6
- out_grad: bfloat16 [64, 16, 64, 2560], P('group', 'row'), may hold values from -6 to 6
- slots: int32 [64, 16, 64], P('group', 'row'), may hold values from 0 to 7
- decay: float32 [20], replicated, may hold values from 0.3 to 0.95
Outputs:
- query_grad: bfloat16 [64, 16, 64, 2560], P('group', 'row')
- key_grad: bfloat16 [64, 16, 64, 2560], P('group', 'row')
- value_grad: bfloat16 [64, 16, 64, 2560], P('group', 'row')
The draws below stay inside these ranges and needn't reach their ends.
All inputs are finite; a program needn't handle non-finite values.
Results may differ from the reference program's by a relative error of at most 0.025.
Values may be sent and summed in bfloat16 or wider, within the bound.
A program may use at most 128 MiB of HBM per device.

```python
import math
import jax
import jax.numpy as jnp
from jax import lax

H = 20
E = 128
S = 8
F = 2
C = 64
FRAMES = 64
ROWS = 16
SW = 4
N_GROUP = 32
N_ROW = 16


def draw_queries(key, part):
    shape = (FRAMES, ROWS, C, H * E)
    key = jax.random.fold_in(key, 1)
    return jnp.clip(jax.random.normal(key, shape, jnp.float32), -5.0, 5.0).astype(jnp.bfloat16)


def draw_keys(key, part):
    shape = (FRAMES, ROWS, C, H * E)
    key = jax.random.fold_in(key, 2)
    return jnp.clip(jax.random.normal(key, shape, jnp.float32), -5.0, 5.0).astype(jnp.bfloat16)


def plant(array, own_key, least, high):
    longest = array.shape.index(max(array.shape))
    spots = []
    for shift in (0, 1):
        where = [jax.random.randint(jax.random.fold_in(own_key, axis), (), 0, length) for axis, length in enumerate(array.shape)]
        where[longest] = (where[longest] + shift) % array.shape[longest]
        spots.append(tuple(where))
    return array.at[spots[0]].set(least).at[spots[1]].set(high)


def levels(stream_key, shape, shards, smallest, high):
    level = 1.0
    for position, parts in shards:
        draws = jax.random.uniform(jax.random.fold_in(jax.random.fold_in(stream_key, 6), position), (parts,), jnp.float32, smallest / len(shards), high / len(shards))
        level = level * jnp.repeat(jnp.exp(draws), shape[position] // parts).reshape((-1,) + (1,) * (len(shape) - 1 - position))
    return level


def scatter_about(stream_key, extent, spread, bound, cuts=(), kind=jnp.bfloat16):
    drawn = jax.random.normal(stream_key, extent, jnp.float32) * spread
    if len(cuts) > 0:
        drawn = levels(stream_key, extent, cuts, -0.22, 0.18) * drawn
    return jnp.clip(drawn, min=-bound, max=bound).astype(kind)


def setup_inputs(seed: int = 0) -> dict:
    streams_of = jax.random.split(jax.random.key(seed), 7)
    return {
        "queries": draw_queries(jax.random.fold_in(streams_of[6], 71), 0),
        "keys": draw_keys(jax.random.fold_in(streams_of[6], 71), 0),
        "values": scatter_about(streams_of[2], (FRAMES, ROWS, C, H * E), 1.0, 6.0, ((0, 32), (1, 16))),
        "out_grad": scatter_about(streams_of[3], (FRAMES, ROWS, C, H * E), 1.0, 6.0, ((0, 32), (1, 16))),
        "slots": plant(jax.random.randint(streams_of[4], (FRAMES, ROWS, C), 0, S), jax.random.fold_in(streams_of[4], 1), 0, S - 1).astype(jnp.int32),
        "decay": jnp.clip(jnp.exp(jax.random.uniform(streams_of[5], (H,), jnp.float32, math.log(0.3), math.log(0.95))), 0.3, 0.95),
    }


def attend(queries, keys, values, valid, grads):
    scale = queries.shape[-1] ** (-0.5)
    qf = queries.astype(jnp.float32)
    kf = keys.astype(jnp.float32)
    vf = values.astype(jnp.float32)
    gf = grads.astype(jnp.float32)
    scores = jnp.einsum('bqhe,bkhe->bhqk', qf, kf) * scale
    scores = jnp.where(valid[:, None, None, :], scores, -1e+30)
    top = lax.optimization_barrier(jnp.max(scores, axis=-1, keepdims=True))
    weights = jnp.exp(scores - top)
    probs = weights / lax.optimization_barrier(jnp.sum(weights, axis=-1, keepdims=True))
    probs_b = lax.optimization_barrier(probs.astype(jnp.bfloat16)).astype(jnp.float32)
    output = jnp.einsum('bhqk,bkhe->bqhe', probs_b, vf)
    delta = jnp.einsum('bqhe,bqhe->bhq', gf, output)
    dprob = jnp.einsum('bqhe,bkhe->bhqk', gf, vf)
    dscore = probs * (dprob - delta[..., None]) * scale
    dscore = lax.optimization_barrier(dscore.astype(jnp.bfloat16)).astype(jnp.float32)
    dq = jnp.einsum('bhqk,bkhe->bqhe', dscore, kf)
    dk = jnp.einsum('bhqk,bqhe->bkhe', dscore, qf)
    dv = jnp.einsum('bhqk,bqhe->bkhe', probs_b, gf)
    return (dq, dk, dv)

def row_windows(field):
    frames, rows, width, feats = field.shape
    padded = jnp.pad(field, ((0, 0), (1, 1), (0, 0), (0, 0)))
    stacked = jnp.stack([padded[:, i:i + rows] for i in range(3)], axis=2)
    stacked = jnp.transpose(stacked, (1, 0, 2, 3, 4))
    return stacked.reshape(rows, frames * 3 * width, H // 2, E)

def col_windows(field):
    frames, rows, width, feats = field.shape
    blocks = field.reshape(frames, rows, N_ROW, SW, feats)
    padded = jnp.pad(blocks, ((0, 0), (0, 0), (1, 1), (0, 0), (0, 0)))
    stacked = jnp.stack([padded[:, :, i:i + N_ROW] for i in range(3)], axis=3)
    stacked = jnp.transpose(stacked, (2, 0, 1, 3, 4, 5))
    return stacked.reshape(N_ROW, frames * rows * 3 * SW, H // 2, E)

def reference(queries, keys, values, out_grad, slots, decay):
    feats = H * E
    half = H // 2 * E
    shape5 = (N_GROUP, F, N_ROW, C, feats)
    qs = queries.reshape(shape5)
    ks = keys.reshape(shape5)
    vs = values.reshape(shape5)
    gs = out_grad.reshape(shape5)
    onehot = (slots.reshape(N_GROUP, F, N_ROW, C)[..., None] == jnp.arange(S, dtype=jnp.int32)).astype(jnp.float32)
    counts = lax.optimization_barrier(jnp.sum(onehot, axis=(1, 2, 3)))
    inv_norm = 1.0 / jnp.sqrt(jnp.maximum(counts, 1.0))

    def pool_group(args):
        kc, vc, oh = args
        ohf = oh.reshape(-1, S)
        sk = jnp.dot(ohf.T, kc.astype(jnp.float32).reshape(-1, feats), precision=lax.Precision.HIGHEST)
        sv = jnp.dot(ohf.T, vc.astype(jnp.float32).reshape(-1, feats), precision=lax.Precision.HIGHEST)
        return (sk, sv)
    sum_k, sum_v = lax.map(pool_group, (ks, vs, onehot))
    pooled_k = sum_k * inv_norm[..., None]
    pooled_v = sum_v * inv_norm[..., None]
    rate = jnp.repeat(decay, E)

    def recur(pk, pv):

        def step(carry, item):
            mk, mv = carry
            return ((rate * mk + item[0], rate * mv + item[1]), (mk, mv))
        start = jnp.zeros((S, feats), jnp.float32)
        _, mems = lax.scan(step, (start, start), (pk, pv))
        return mems
    (mems_k, mems_v), recur_back = jax.vjp(recur, pooled_k, pooled_v)
    mem_kb = mems_k.astype(jnp.bfloat16)
    mem_vb = mems_v.astype(jnp.bfloat16)
    idx = jnp.arange(N_ROW)
    flags = jnp.stack([idx > 0, idx >= 0, idx < N_ROW - 1], axis=1)
    valid_row = jnp.broadcast_to(flags[:, None, :, None], (N_ROW, F, 3, C)).reshape(N_ROW, -1)
    valid_col = jnp.broadcast_to(flags[:, None, None, :, None], (N_ROW, F, N_ROW, 3, SW)).reshape(N_ROW, -1)
    mem_valid = jnp.ones((N_ROW, S), dtype=bool)

    def group_grads(args):
        qc, kc, vc, gc, mk, mv = args

        def windows(kx, vx):
            return (row_windows(kx[..., :half]), row_windows(vx[..., :half]), col_windows(kx[..., half:]), col_windows(vx[..., half:]))
        wins, back = jax.vjp(windows, kc.astype(jnp.float32), vc.astype(jnp.float32))
        q_row = jnp.transpose(qc[..., :half], (1, 0, 2, 3)).reshape(N_ROW, F * C, H // 2, E)
        g_row = jnp.transpose(gc[..., :half], (1, 0, 2, 3)).reshape(N_ROW, F * C, H // 2, E)
        q_col = jnp.transpose(qc[..., half:].reshape(F, N_ROW, N_ROW, SW, half), (2, 0, 1, 3, 4)).reshape(N_ROW, F * N_ROW * SW, H // 2, E)
        g_col = jnp.transpose(gc[..., half:].reshape(F, N_ROW, N_ROW, SW, half), (2, 0, 1, 3, 4)).reshape(N_ROW, F * N_ROW * SW, H // 2, E)
        nk = wins[0].shape[1]

        def with_memory(win, mem):
            extra = jnp.broadcast_to(mem.reshape(1, S, H // 2, E), (N_ROW, S, H // 2, E))
            return jnp.concatenate([win.astype(jnp.bfloat16), extra], axis=1)
        dq_r, dk_r, dv_r = attend(q_row, with_memory(wins[0], mk[:, :half]), with_memory(wins[1], mv[:, :half]), jnp.concatenate([valid_row, mem_valid], axis=1), g_row)
        dq_c, dk_c, dv_c = attend(q_col, with_memory(wins[2], mk[:, half:]), with_memory(wins[3], mv[:, half:]), jnp.concatenate([valid_col, mem_valid], axis=1), g_col)
        dk_dir, dv_dir = back((dk_r[:, :nk], dv_r[:, :nk], dk_c[:, :nk], dv_c[:, :nk]))
        dmk = jnp.concatenate([lax.optimization_barrier(jnp.sum(dk_r[:, nk:], axis=0)).reshape(S, half), lax.optimization_barrier(jnp.sum(dk_c[:, nk:], axis=0)).reshape(S, half)], axis=1)
        dmv = jnp.concatenate([lax.optimization_barrier(jnp.sum(dv_r[:, nk:], axis=0)).reshape(S, half), lax.optimization_barrier(jnp.sum(dv_c[:, nk:], axis=0)).reshape(S, half)], axis=1)
        dq_rows = jnp.transpose(dq_r.reshape(N_ROW, F, C, half), (1, 0, 2, 3))
        dq_cols = jnp.transpose(dq_c.reshape(N_ROW, F, N_ROW, SW, half), (1, 2, 0, 3, 4)).reshape(F, N_ROW, C, half)
        dq = jnp.concatenate([dq_rows, dq_cols], axis=-1).astype(jnp.bfloat16)
        return (dq, dk_dir, dv_dir, dmk, dmv)
    dq_all, dk_dir, dv_dir, dmem_k, dmem_v = lax.map(group_grads, (qs, ks, vs, gs, mem_kb, mem_vb))
    dpool_k, dpool_v = recur_back((dmem_k, dmem_v))

    def finish(args):
        dkd, dvd, oh, pk, pv = args
        add_k = jnp.einsum('frcs,sd->frcd', oh, pk, precision=lax.Precision.HIGHEST)
        add_v = jnp.einsum('frcs,sd->frcd', oh, pv, precision=lax.Precision.HIGHEST)
        return ((dkd + add_k).astype(jnp.bfloat16), (dvd + add_v).astype(jnp.bfloat16))
    dk_all, dv_all = lax.map(finish, (dk_dir, dv_dir, onehot, dpool_k * inv_norm[..., None], dpool_v * inv_norm[..., None]))
    full = (FRAMES, ROWS, C, feats)
    return (dq_all.reshape(full), dk_all.reshape(full), dv_all.reshape(full))
```

```python
import jax
import jax.numpy as jnp
from jax import lax
from jax.experimental import pallas as pl
from jax.experimental.pallas import tpu as pltpu
from jax.sharding import PartitionSpec as P

S = 8
E = 128
TOKENS = 128
HALF = 1280
PART = 640
FEATS = 2560
ROWS = 16
MESH = pl.DeviceIdType.MESH
F32 = jnp.float32
BF16 = jnp.bfloat16
NEG = -1e30


def select(rows, cols, source):
    o = lax.broadcasted_iota(jnp.int32, (rows, cols), 0)
    i = lax.broadcasted_iota(jnp.int32, (rows, cols), 1)
    return jnp.where(source(o) == i, 1.0, 0.0).astype(BF16)


def select_back(rows, cols, source):
    i = lax.broadcasted_iota(jnp.int32, (rows, cols), 0)
    o = lax.broadcasted_iota(jnp.int32, (rows, cols), 1)
    return jnp.where(source(o) == i, 1.0, 0.0).astype(BF16)


def by_pair(s):
    return ((s >> 3) & 1) * 64 + (s >> 4) * 8 + (s & 7)


def by_stripe(o):
    return ((o >> 3) & 15) * 16 + ((o >> 2) & 1) * 8 + (o >> 7) * 4 + (o & 3)


def dot(a, b, ca=1, cb=0):
    return lax.dot_general(a, b, (((ca,), (cb,)), ((), ())), preferred_element_type=F32)


def unit(q, g, keys, values, low, high):
    scale = E ** (-0.5)
    s = dot(keys, q, 1, 1) * scale
    used = lax.broadcasted_iota(jnp.int32, (16, 128), 0) < S
    s = jnp.concatenate(
        [s[:128] + low, s[128:256], s[256:384] + high, jnp.where(used, s[384:], NEG)], axis=0
    )
    top = jnp.max(s, axis=0, keepdims=True)
    w = jnp.exp(s - top)
    p = w * (1.0 / jnp.sum(w, axis=0, keepdims=True))
    pb = p.astype(BF16)
    dprob = dot(values, g, 1, 1)
    delta = jnp.sum(pb.astype(F32) * dprob, axis=0, keepdims=True)
    ds = (p * ((dprob - delta) * scale)).astype(BF16)
    dk = dot(ds, q)
    dv = dot(pb, g)
    dq = dot(ds, keys, 0, 0)
    return dq, dk, dv


def kernel(
    q_ref, k_ref, v_ref, g_ref, slots_ref, decay_ref,
    oq_ref, ok_ref, ov_ref,
    ms, rs, zp, zb, bp, bt, mp, mem, memk, memv,
    ms2, rs2, zp2, zb2, bp2, bt2, mp2, mem2,
    m2, dm,
    cs, cr, sep, hr, hc, gs, gr, own, cown, cgs, cgr,
    bsq, bskv, brq, brkv,
    send, recv,
):
    r = lax.axis_index("row")
    n = lax.axis_index("group")
    blk = n // 8
    idx = n % 8
    x = r // 4
    y = r % 4
    hh = y % 2
    yh = y // 2
    jp = x + yh * (7 - 2 * x)

    def holder(pair, part):
        high = pair // 4
        low = pair % 4
        return (low + high * (3 - 2 * low)) * 4 + high * 2 + part

    def in_row(d):
        return lax.rem(r + d, ROWS)

    def in_block(d):
        return blk * 8 + lax.rem(idx + d, 8)

    def in_blocks(d):
        return lax.rem(blk + d, 4) * 8 + idx

    barrier = pltpu.get_barrier_semaphore()

    def greet(axis, pick, count):
        def body(d, c):
            pl.semaphore_signal(barrier, inc=1, device_id={axis: pick(d)}, device_id_type=MESH)
            return c

        lax.fori_loop(1, count, body, 0)

    greet("row", in_row, ROWS)
    greet("group", in_block, 8)
    greet("group", in_blocks, 4)

    def push(src, dst, k, device):
        pltpu.make_async_remote_copy(
            src_ref=src, dst_ref=dst, send_sem=send.at[k], recv_sem=recv.at[k],
            device_id=device, device_id_type=MESH,
        ).start()

    def arrived(shape_of, k):
        pltpu.make_async_copy(shape_of, shape_of, recv.at[k]).wait()

    def left(shape_of, k):
        pltpu.make_async_copy(shape_of, shape_of, send.at[k]).wait()

    def push_all(axis, pick, count, src, dst, k):
        def body(d, c):
            t = pick(d)
            push(src(t), dst, k, {axis: t})
            return c

        lax.fori_loop(1, count, body, 0)

    slot_iota = lax.broadcasted_iota(jnp.int32, (S, 64), 0)
    member = [jnp.where(slots_ref[f] == slot_iota, 1.0, 0.0) for f in range(2)]
    member_b = [m.astype(BF16) for m in member]
    count = jnp.sum(member[0] + member[1], axis=1, keepdims=True)
    for a, ref in enumerate((k_ref, v_ref)):
        total = dot(member_b[0], ref[0:64, :]) + dot(member_b[1], ref[64:128, :])
        for s in range(S):
            ms[a * S + s, :, 0:FEATS] = total[s : s + 1]
            ms[a * S + s, :, FEATS:] = jnp.broadcast_to(count[s : s + 1], (1, 128))
    rs[r] = ms[r]

    to_pair = select(128, 128, by_pair)

    def arrange(h, c):
        ln = pl.ds(pl.multiple_of(h * 256, 256), 256)
        wide = pl.ds(pl.multiple_of(HALF + h * 256, 256), 256)
        for a, ref in enumerate((q_ref, k_ref, v_ref, g_ref)):
            cs[:, a, :, ln] = dot(to_pair, ref[:, wide]).astype(BF16).reshape(8, 16, 256)
        return c

    lax.fori_loop(0, 5, arrange, 0)
    mine = pl.ds(pl.multiple_of(hh * PART, 128), PART)
    cr[r] = cs[jp, :, :, mine]

    pl.semaphore_wait(barrier, 15 + 7 + 3)

    push_all("row", in_row, ROWS, lambda t: ms.at[t], rs.at[r], 0)

    before = lax.rem(r + ROWS - 1, ROWS)
    after = lax.rem(r + 1, ROWS)
    rows_half = (slice(None), pl.ds(0, HALF))
    push(k_ref.at[rows_half], hr.at[1, 0], 5, {"row": before})
    push(v_ref.at[rows_half], hr.at[1, 1], 6, {"row": before})
    push(k_ref.at[rows_half], hr.at[0, 0], 7, {"row": after})
    push(v_ref.at[rows_half], hr.at[0, 1], 8, {"row": after})

    def scatter(d, c):
        t = in_row(d)
        tx = t // 4
        ty = t % 4
        tyh = ty // 2
        tjp = tx + tyh * (7 - 2 * tx)
        lanes = pl.ds(pl.multiple_of((ty % 2) * PART, 128), PART)
        push(cs.at[tjp, :, :, lanes], cr.at[r], 4, {"row": t})
        return c

    lax.fori_loop(1, ROWS, scatter, 0)

    log_rate = jnp.log(
        jnp.concatenate([jnp.full((1, 128), decay_ref[h], F32) for h in range(20)], axis=1)
    )

    def power(e, valid):
        return jnp.where(valid, jnp.exp(log_rate * e.astype(F32)), 0.0)

    def combine(rs_, zp_, zb_, bp_, bt_, mp_, mem_, k, forward, norm):
        arrived(rs_.at[pl.ds(0, 15)], k)
        total = jnp.sum(rs_[...], axis=0)
        if norm is None:
            norm = 1.0 / jnp.sqrt(jnp.maximum(total[:, FEATS : FEATS + 1], 1.0))
            piece = total[:, :FEATS] * norm
        else:
            piece = total
        zp_[0] = piece
        zb_[idx] = piece
        push_all("group", in_block, 8, lambda t: zp_.at[0], zb_.at[idx], k + 1)
        arrived(zb_.at[pl.ds(0, 7)], k + 1)
        inside = jnp.zeros((1, FEATS), F32)
        whole = jnp.zeros((1, FEATS), F32)
        for j in range(8):
            got = zb_[j]
            if forward:
                inside = inside + got * power(idx - 1 - j, j < idx)
                whole = whole + got * jnp.exp(log_rate * float(7 - j))
            else:
                inside = inside + got * power(j - idx - 1, j > idx)
                whole = whole + got * jnp.exp(log_rate * float(j))
        bp_[0] = whole
        bt_[blk] = whole
        push_all("group", in_blocks, 4, lambda t: bp_.at[0], bt_.at[blk], k + 2)
        arrived(bt_.at[pl.ds(0, 3)], k + 2)
        for j in range(4):
            if forward:
                inside = inside + bt_[j] * power(8 * (blk - 1 - j) + idx, j < blk)
            else:
                inside = inside + bt_[j] * power(8 * (j - blk - 1) + 7 - idx, j > blk)
        if not forward:
            inside = inside * norm
        mp_[0] = inside
        mem_[r] = inside
        push_all("row", in_row, ROWS, lambda t: mp_.at[0], mem_.at[r], k + 3)
        arrived(mem_.at[pl.ds(0, 15)], k + 3)
        return norm

    norm = combine(rs, zp, zb, bp, bt, mp, mem, 0, True, None)
    zero = jnp.zeros((S, FEATS), F32)
    m2[S:, :] = zero
    for a, to in enumerate((memk, memv)):
        for s in range(S):
            m2[s : s + 1, :] = mem[a * S + s]
        to[...] = m2[...].astype(BF16)
    dm[0] = zero
    dm[1] = zero

    arrived(cr.at[pl.ds(0, 15)], 4)
    to_stripe = select(256, 256, by_stripe)
    for a in (1, 2, 0, 3):
        block = cr[:, a, :, :].reshape(256, PART)
        sep[a] = dot(to_stripe, block).astype(BF16).reshape(2, 128, PART)
    pair_before = holder(lax.rem(jp + 7, 8), hh)
    pair_after = holder(lax.rem(jp + 1, 8), hh)
    push(sep.at[pl.ds(1, 2), 0], hc.at[1], 9, {"row": pair_before})
    push(sep.at[pl.ds(1, 2), 1], hc.at[0], 10, {"row": pair_after})

    for k in (5, 6, 7, 8):
        arrived(hr.at[0, 0], k)
    row_low = jnp.where(r > 0, 0.0, NEG)
    row_high = jnp.where(r < ROWS - 1, 0.0, NEG)

    def row_head(h, c):
        ln = pl.ds(pl.multiple_of(h * E, E), E)
        keys = jnp.concatenate([hr[0, 0, :, ln], k_ref[:, ln], hr[1, 0, :, ln], memk[:, ln]], axis=0)
        vals = jnp.concatenate([hr[0, 1, :, ln], v_ref[:, ln], hr[1, 1, :, ln], memv[:, ln]], axis=0)
        dq, dk, dv = unit(q_ref[:, ln], g_ref[:, ln], keys, vals, row_low, row_high)
        oq_ref[:, ln] = dq.astype(BF16)
        for a, d in enumerate((dk, dv)):
            gs[0, a, :, ln] = d[0:128].astype(BF16)
            own[a, :, ln] = d[128:256]
            gs[1, a, :, ln] = d[256:384].astype(BF16)
            dm[a, :, ln] = d[384:392]
        return c

    lax.fori_loop(0, 10, row_head, 0)
    push(gs.at[0], gr.at[1], 11, {"row": before})
    push(gs.at[1], gr.at[0], 12, {"row": after})

    arrived(hc.at[1], 9)
    arrived(hc.at[0], 10)
    col_low = jnp.where(jp > 0, 0.0, NEG)
    col_high = jnp.where(jp < 7, 0.0, NEG)

    def col_head(h, c):
        ln = pl.ds(pl.multiple_of(h * E, E), E)
        wide = pl.ds(pl.multiple_of(HALF + hh * PART + h * E, E), E)
        mk = memk[:, wide]
        mv = memv[:, wide]
        k0, k1, k2, k3 = hc[0, 0, :, ln], sep[1, 0, :, ln], sep[1, 1, :, ln], hc[1, 0, :, ln]
        v0, v1, v2, v3 = hc[0, 1, :, ln], sep[2, 0, :, ln], sep[2, 1, :, ln], hc[1, 1, :, ln]
        qa, ka, va = unit(
            sep[0, 0, :, ln], sep[3, 0, :, ln],
            jnp.concatenate([k0, k1, k2, mk], axis=0), jnp.concatenate([v0, v1, v2, mv], axis=0),
            col_low, 0.0,
        )
        for a, d in enumerate((ka, va)):
            cgs[0, a, :, ln] = d[0:128].astype(BF16)
            cown[a, :, ln] = d[128:384]
            dm[a, :, wide] = d[384:392]
        sep[0, 0, :, ln] = qa.astype(BF16)
        qb, kb, vb = unit(
            sep[0, 1, :, ln], sep[3, 1, :, ln],
            jnp.concatenate([k1, k2, k3, mk], axis=0), jnp.concatenate([v1, v2, v3, mv], axis=0),
            0.0, col_high,
        )
        for a, d in enumerate((kb, vb)):
            cgs[1, a, :, ln] = d[256:384].astype(BF16)
            cown[a, :, ln] = cown[a, :, ln] + d[0:256]
            dm[a, :, wide] = dm[a, :, wide] + d[384:392]
        sep[0, 1, :, ln] = qb.astype(BF16)
        return c

    lax.fori_loop(0, 5, col_head, 0)

    for a in range(2):
        for s in range(S):
            ms2[a * S + s] = dm[a, s : s + 1, :]
    rs2[r] = ms2[r]
    push_all("row", in_row, ROWS, lambda t: ms2.at[t], rs2.at[r], 15)
    push(cgs.at[0], cgr.at[1], 13, {"row": pair_before})
    push(cgs.at[1], cgr.at[0], 14, {"row": pair_after})

    from_stripe = select_back(256, 256, by_stripe)
    bsq[...] = dot(from_stripe, sep[0].reshape(256, PART)).astype(BF16).reshape(16, 16, PART)
    brq[jp, :, mine] = bsq[r]
    push_all("row", in_row, ROWS, lambda t: bsq.at[t], brq.at[jp, :, mine], 19)

    arrived(cgr.at[1], 13)
    arrived(cgr.at[0], 14)
    for a in range(2):
        full = jnp.concatenate(
            [
                cown[a, 0:128, :] + cgr[0, a].astype(F32),
                cown[a, 128:256, :] + cgr[1, a].astype(F32),
            ],
            axis=0,
        ).astype(BF16)
        bskv[:, a, :, :] = dot(from_stripe, full).astype(BF16).reshape(16, 16, PART)
    brkv[jp, :, :, mine] = bskv[r]
    push_all("row", in_row, ROWS, lambda t: bskv.at[t], brkv.at[jp, :, :, mine], 20)

    combine(rs2, zp2, zb2, bp2, bt2, mp2, mem2, 15, False, norm)
    for a in range(2):
        for s in range(S):
            dm[a, s : s + 1, :] = mem2[a * S + s]

    arrived(gr.at[1], 11)
    arrived(gr.at[0], 12)
    arrived(bsq.at[pl.ds(0, 15)], 19)
    arrived(bskv.at[pl.ds(0, 15)], 20)
    from_pair = select_back(128, 128, by_pair)

    def finish(h, c):
        ln = pl.ds(pl.multiple_of(h * E, E), E)
        wide = pl.ds(pl.multiple_of(HALF + h * E, E), E)
        oq_ref[:, wide] = dot(from_pair, brq[:, :, ln].reshape(128, E)).astype(BF16)
        for a, out in enumerate((ok_ref, ov_ref)):
            back = dot(from_pair, brkv[:, a, :, ln].reshape(128, E))
            dr = dm[a, :, ln].astype(BF16)
            dc = dm[a, :, wide].astype(BF16)
            add_r = jnp.concatenate([dot(member_b[f], dr, 0, 0) for f in range(2)], axis=0)
            add_c = jnp.concatenate([dot(member_b[f], dc, 0, 0) for f in range(2)], axis=0)
            near = gr[0, a, :, ln].astype(F32) + gr[1, a, :, ln].astype(F32)
            out[:, ln] = (own[a, :, ln] + near + add_r).astype(BF16)
            out[:, wide] = (back + add_c).astype(BF16)
        return c

    lax.fori_loop(0, 10, finish, 0)

    left(ms.at[pl.ds(0, 15)], 0)
    left(zb.at[pl.ds(0, 7)], 1)
    left(bt.at[pl.ds(0, 3)], 2)
    left(mem.at[pl.ds(0, 15)], 3)
    left(cr.at[pl.ds(0, 15)], 4)
    for k in (5, 6, 7, 8):
        left(hr.at[0, 0], k)
    left(hc.at[1], 9)
    left(hc.at[0], 10)
    left(gs.at[0], 11)
    left(gs.at[1], 12)
    left(cgs.at[0], 13)
    left(cgs.at[1], 14)
    left(ms2.at[pl.ds(0, 15)], 15)
    left(zb2.at[pl.ds(0, 7)], 16)
    left(bt2.at[pl.ds(0, 3)], 17)
    left(mem2.at[pl.ds(0, 15)], 18)
    left(bsq.at[pl.ds(0, 15)], 19)
    left(bskv.at[pl.ds(0, 15)], 20)


def per_device(queries, keys, values, out_grad, slots, decay):
    flat = (TOKENS, FEATS)
    vm = pl.BlockSpec(memory_space=pltpu.VMEM)

    def row(count, width=FEATS):
        return pltpu.VMEM((count, 1, width), F32)

    scratch = [
        row(16, FEATS + 128), row(16, FEATS + 128),
        row(1), row(8), row(1), row(4), row(1), row(16),
        pltpu.VMEM((16, FEATS), BF16), pltpu.VMEM((16, FEATS), BF16),
        row(16), row(16),
        row(1), row(8), row(1), row(4), row(1), row(16),
        pltpu.VMEM((16, FEATS), F32), pltpu.VMEM((2, S, FEATS), F32),
        pltpu.VMEM((8, 4, 16, HALF), BF16),
        pltpu.VMEM((16, 4, 16, PART), BF16),
        pltpu.VMEM((4, 2, 128, PART), BF16),
        pltpu.VMEM((2, 2, 128, HALF), BF16),
        pltpu.VMEM((2, 2, 128, PART), BF16),
        pltpu.VMEM((2, 2, 128, HALF), BF16),
        pltpu.VMEM((2, 2, 128, HALF), BF16),
        pltpu.VMEM((2, 128, HALF), F32),
        pltpu.VMEM((2, 256, PART), F32),
        pltpu.VMEM((2, 2, 128, PART), BF16),
        pltpu.VMEM((2, 2, 128, PART), BF16),
        pltpu.VMEM((16, 16, PART), BF16),
        pltpu.VMEM((16, 2, 16, PART), BF16),
        pltpu.VMEM((8, 16, HALF), BF16),
        pltpu.VMEM((8, 2, 16, HALF), BF16),
        pltpu.SemaphoreType.DMA((21,)),
        pltpu.SemaphoreType.DMA((21,)),
    ]
    outs = pl.pallas_call(
        kernel,
        out_shape=[jax.ShapeDtypeStruct(flat, BF16)] * 3,
        in_specs=[vm] * 5 + [pl.BlockSpec(memory_space=pltpu.SMEM)],
        out_specs=[vm] * 3,
        scratch_shapes=scratch,
        compiler_params=pltpu.CompilerParams(
            collective_id=0, has_side_effects=True, vmem_limit_bytes=48 * 1024 * 1024
        ),
    )(
        queries.reshape(flat), keys.reshape(flat), values.reshape(flat), out_grad.reshape(flat),
        slots, decay,
    )
    return tuple(o.reshape(queries.shape) for o in outs)


def solution(mesh):
    spec = P("group", "row", None, None)
    return jax.shard_map(
        per_device,
        mesh=mesh,
        in_specs=(spec, spec, spec, spec, P("group", "row", None), P()),
        out_specs=(spec, spec, spec),
        check_vma=False,
    )
```

```python
import jax
import jax.numpy as jnp
from jax import lax
from jax.experimental import pallas as pl
from jax.experimental.pallas import tpu as pltpu
from jax.sharding import PartitionSpec as P

S = 8
E = 128
TOKENS = 128
HALF = 1280
PART = 640
FEATS = 2560
ROWS = 16
MESH = pl.DeviceIdType.MESH
F32 = jnp.float32
BF16 = jnp.bfloat16
NEG = -1e30


def select(rows, cols, source):
    o = lax.broadcasted_iota(jnp.int32, (rows, cols), 0)
    i = lax.broadcasted_iota(jnp.int32, (rows, cols), 1)
    return jnp.where(source(o) == i, 1.0, 0.0).astype(BF16)


def select_back(rows, cols, source):
    i = lax.broadcasted_iota(jnp.int32, (rows, cols), 0)
    o = lax.broadcasted_iota(jnp.int32, (rows, cols), 1)
    return jnp.where(source(o) == i, 1.0, 0.0).astype(BF16)


def by_pair(s):
    return ((s >> 3) & 1) * 64 + (s >> 4) * 8 + (s & 7)


def by_stripe(o):
    return ((o >> 3) & 15) * 16 + ((o >> 2) & 1) * 8 + (o >> 7) * 4 + (o & 3)


def dot(a, b, ca=1, cb=0):
    return lax.dot_general(a, b, (((ca,), (cb,)), ((), ())), preferred_element_type=F32)


def unit(q, g, keys, values, low, high):
    scale = E ** (-0.5)
    s = dot(keys, q, 1, 1) * scale
    used = lax.broadcasted_iota(jnp.int32, (16, 128), 0) < S
    s = jnp.concatenate(
        [s[:128] + low, s[128:256], s[256:384] + high, jnp.where(used, s[384:], NEG)], axis=0
    )
    top = jnp.max(s, axis=0, keepdims=True)
    w = jnp.exp(s - top)
    p = w * (1.0 / jnp.sum(w, axis=0, keepdims=True))
    pb = p.astype(BF16)
    dprob = dot(values, g, 1, 1)
    delta = jnp.sum(pb.astype(F32) * dprob, axis=0, keepdims=True)
    ds = (p * ((dprob - delta) * scale)).astype(BF16)
    dk = dot(ds, q)
    dv = dot(pb, g)
    dq = dot(ds, keys, 0, 0)
    return dq, dk, dv


def kernel(
    qh_ref, kh_ref, vh_ref, gh_ref, slots_ref, decay_ref,
    oq_ref, ok_ref, ov_ref,
    q_ref, k_ref, v_ref, g_ref, wts,
    ms, rs, zp, zb, bp, bt, mp, mem, memk, memv,
    ms2, rs2, zp2, zb2, bp2, bt2, mp2, mem2,
    m2, dm,
    cskv, csqg, crkv, crqg, sep, hr, hc, gs, gr, own, cown, cgs, cgr,
    bsq, bskv, brq, brkv,
    send, recv, load,
):
    r = lax.axis_index("row")
    n = lax.axis_index("group")
    blk = n // 8
    idx = n % 8
    x = r // 4
    y = r % 4
    hh = y % 2
    yh = y // 2
    jp = x + yh * (7 - 2 * x)

    def holder(pair, part):
        high = pair // 4
        low = pair % 4
        return (low + high * (3 - 2 * low)) * 4 + high * 2 + part

    def in_row(d):
        return lax.rem(r + d, ROWS)

    def in_block(d):
        return blk * 8 + lax.rem(idx + d, 8)

    def in_blocks(d):
        return lax.rem(blk + d, 4) * 8 + idx

    barrier = pltpu.get_barrier_semaphore()

    def greet(axis, pick, count):
        def body(d, c):
            pl.semaphore_signal(barrier, inc=1, device_id={axis: pick(d)}, device_id_type=MESH)
            return c

        lax.fori_loop(1, count, body, 0)

    greet("row", in_row, ROWS)
    greet("group", in_block, 8)
    greet("group", in_blocks, 4)

    pairs = ((kh_ref, k_ref), (vh_ref, v_ref), (qh_ref, q_ref), (gh_ref, g_ref))

    def fetch(a, part):
        cols = (slice(None), pl.ds(part * HALF, HALF))
        return pltpu.make_async_copy(
            pairs[a][0].at[cols], pairs[a][1].at[cols], load.at[a * 2 + part]
        )

    for part in (1, 0):
        for a in range(4):
            fetch(a, part).start()

    def push(src, dst, k, device):
        pltpu.make_async_remote_copy(
            src_ref=src, dst_ref=dst, send_sem=send.at[k], recv_sem=recv.at[k],
            device_id=device, device_id_type=MESH,
        ).start()

    def arrived(shape_of, k):
        pltpu.make_async_copy(shape_of, shape_of, recv.at[k]).wait()

    def left(shape_of, k):
        pltpu.make_async_copy(shape_of, shape_of, send.at[k]).wait()

    def push_all(axis, pick, count, src, dst, k):
        def body(d, c):
            t = pick(d)
            push(src(t), dst, k, {axis: t})
            return c

        lax.fori_loop(1, count, body, 0)

    to_pair = select(128, 128, by_pair)
    mine = pl.ds(pl.multiple_of(hh * PART, 128), PART)

    def arrange(first, second, to):
        def body(h, c):
            ln = pl.ds(pl.multiple_of(h * 256, 256), 256)
            wide = pl.ds(pl.multiple_of(HALF + h * 256, 256), 256)
            for a, ref in enumerate((first, second)):
                to[:, a, :, ln] = dot(to_pair, ref[:, wide]).astype(BF16).reshape(8, 16, 256)
            return c

        lax.fori_loop(0, 5, body, 0)

    fetch(0, 1).wait()
    fetch(1, 1).wait()
    arrange(k_ref, v_ref, cskv)
    crkv[r] = cskv[jp, :, :, mine]
    fetch(2, 1).wait()
    fetch(3, 1).wait()
    arrange(q_ref, g_ref, csqg)
    crqg[r] = csqg[jp, :, :, mine]

    fetch(0, 0).wait()
    fetch(1, 0).wait()
    slot_iota = lax.broadcasted_iota(jnp.int32, (S, 64), 0)
    member = [jnp.where(slots_ref[f] == slot_iota, 1.0, 0.0) for f in range(2)]
    member_b = [m.astype(BF16) for m in member]
    count = jnp.sum(member[0] + member[1], axis=1, keepdims=True)
    for a, ref in enumerate((k_ref, v_ref)):
        total = dot(member_b[0], ref[0:64, :]) + dot(member_b[1], ref[64:128, :])
        for s in range(S):
            ms[a * S + s, :, 0:FEATS] = total[s : s + 1]
            ms[a * S + s, :, FEATS:] = jnp.broadcast_to(count[s : s + 1], (1, 128))
    rs[r] = ms[r]

    log_rate = jnp.log(
        jnp.concatenate([jnp.full((1, 128), decay_ref[h], F32) for h in range(20)], axis=1)
    )

    def power(e):
        return jnp.exp(log_rate * e.astype(F32))

    for j in range(8):
        wts[j] = jnp.where(j < idx, power(idx - 1 - j), 0.0)
        wts[8 + j] = jnp.exp(log_rate * float(7 - j))
        wts[20 + j] = jnp.where(j > idx, power(j - idx - 1), 0.0)
        wts[28 + j] = jnp.exp(log_rate * float(j))
    for j in range(4):
        wts[16 + j] = jnp.where(j < blk, power(8 * (blk - 1 - j) + idx), 0.0)
        wts[36 + j] = jnp.where(j > blk, power(8 * (j - blk - 1) + 7 - idx), 0.0)

    fetch(2, 0).wait()
    fetch(3, 0).wait()
    pl.semaphore_wait(barrier, 15 + 7 + 3)

    def scatter(source, to, k):
        def body(d, c):
            t = in_row(d)
            tx = t // 4
            ty = t % 4
            tyh = ty // 2
            tjp = tx + tyh * (7 - 2 * tx)
            lanes = pl.ds(pl.multiple_of((ty % 2) * PART, 128), PART)
            push(source.at[tjp, :, :, lanes], to.at[r], k, {"row": t})
            return c

        lax.fori_loop(1, ROWS, body, 0)

    push_all("row", in_row, ROWS, lambda t: ms.at[t], rs.at[r], 0)
    scatter(cskv, crkv, 4)
    scatter(csqg, crqg, 21)

    def to_the_block(piece, zp_, zb_, k):
        zp_[0] = piece
        zb_[idx] = piece
        push_all("group", in_block, 8, lambda t: zp_.at[0], zb_.at[idx], k)

    def to_the_blocks(zb_, bp_, bt_, k, first):
        arrived(zb_.at[pl.ds(0, 7)], k - 1)
        whole = jnp.sum(zb_[...] * wts[first + 8 : first + 16], axis=0)
        bp_[0] = whole
        bt_[blk] = whole
        push_all("group", in_blocks, 4, lambda t: bp_.at[0], bt_.at[blk], k)
        return jnp.sum(zb_[...] * wts[first : first + 8], axis=0)

    def to_the_row(inside, bt_, mp_, mem_, k, first, norm_):
        arrived(bt_.at[pl.ds(0, 3)], k - 1)
        inside = inside + jnp.sum(bt_[...] * wts[first + 16 : first + 20], axis=0)
        if norm_ is not None:
            inside = inside * norm_
        mp_[0] = inside
        mem_[r] = inside
        push_all("row", in_row, ROWS, lambda t: mp_.at[0], mem_.at[r], k)

    arrived(rs.at[pl.ds(0, 15)], 0)
    total = jnp.sum(rs[...], axis=0)
    norm = 1.0 / jnp.sqrt(jnp.maximum(total[:, FEATS : FEATS + 1], 1.0))
    to_the_block(total[:, :FEATS] * norm, zp, zb, 1)

    to_stripe = select(256, 256, by_stripe)

    def split(from_, a, to):
        block = from_[:, a, :, :].reshape(256, PART)
        sep[to] = dot(to_stripe, block).astype(BF16).reshape(2, 128, PART)

    pair_before = holder(lax.rem(jp + 7, 8), hh)
    pair_after = holder(lax.rem(jp + 1, 8), hh)
    arrived(crkv.at[pl.ds(0, 15)], 4)
    split(crkv, 0, 1)
    split(crkv, 1, 2)
    push(sep.at[pl.ds(1, 2), 0], hc.at[1], 9, {"row": pair_before})
    push(sep.at[pl.ds(1, 2), 1], hc.at[0], 10, {"row": pair_after})

    inside = to_the_blocks(zb, bp, bt, 2, 0)
    to_the_row(inside, bt, mp, mem, 3, 0, None)

    arrived(crqg.at[pl.ds(0, 15)], 21)
    before = lax.rem(r + ROWS - 1, ROWS)
    after = lax.rem(r + 1, ROWS)
    rows_half = (slice(None), pl.ds(0, HALF))
    push(k_ref.at[rows_half], hr.at[1, 0], 5, {"row": before})
    push(k_ref.at[rows_half], hr.at[0, 0], 7, {"row": after})
    push(v_ref.at[rows_half], hr.at[1, 1], 6, {"row": before})
    push(v_ref.at[rows_half], hr.at[0, 1], 8, {"row": after})
    split(crqg, 0, 0)
    split(crqg, 1, 3)

    arrived(mem.at[pl.ds(0, 15)], 3)
    zero = jnp.zeros((S, FEATS), F32)
    m2[S:, :] = zero
    for a, to in enumerate((memk, memv)):
        for s in range(S):
            m2[s : s + 1, :] = mem[a * S + s]
        to[...] = m2[...].astype(BF16)
    dm[0] = zero
    dm[1] = zero

    arrived(hc.at[1], 9)
    arrived(hc.at[0], 10)
    col_low = jnp.where(jp > 0, 0.0, NEG)
    col_high = jnp.where(jp < 7, 0.0, NEG)

    def col_head(h, c):
        ln = pl.ds(pl.multiple_of(h * E, E), E)
        wide = pl.ds(pl.multiple_of(HALF + hh * PART + h * E, E), E)
        mk = memk[:, wide]
        mv = memv[:, wide]
        k0, k1, k2, k3 = hc[0, 0, :, ln], sep[1, 0, :, ln], sep[1, 1, :, ln], hc[1, 0, :, ln]
        v0, v1, v2, v3 = hc[0, 1, :, ln], sep[2, 0, :, ln], sep[2, 1, :, ln], hc[1, 1, :, ln]
        qa, ka, va = unit(
            sep[0, 0, :, ln], sep[3, 0, :, ln],
            jnp.concatenate([k0, k1, k2, mk], axis=0), jnp.concatenate([v0, v1, v2, mv], axis=0),
            col_low, 0.0,
        )
        qb, kb, vb = unit(
            sep[0, 1, :, ln], sep[3, 1, :, ln],
            jnp.concatenate([k1, k2, k3, mk], axis=0), jnp.concatenate([v1, v2, v3, mv], axis=0),
            0.0, col_high,
        )
        for a, (da, db) in enumerate(((ka, kb), (va, vb))):
            cgs[0, a, :, ln] = da[0:128].astype(BF16)
            cown[a, :, ln] = da[128:384] + db[0:256]
            cgs[1, a, :, ln] = db[256:384].astype(BF16)
            dm[a, :, wide] = da[384:392] + db[384:392]
        sep[0, 0, :, ln] = qa.astype(BF16)
        sep[0, 1, :, ln] = qb.astype(BF16)
        return c

    lax.fori_loop(0, 5, col_head, 0)
    push(cgs.at[0], cgr.at[1], 13, {"row": pair_before})
    push(cgs.at[1], cgr.at[0], 14, {"row": pair_after})
    from_stripe = select_back(256, 256, by_stripe)
    bsq[...] = dot(from_stripe, sep[0].reshape(256, PART)).astype(BF16).reshape(16, 16, PART)
    brq[jp, :, mine] = bsq[r]
    push_all("row", in_row, ROWS, lambda t: bsq.at[t], brq.at[jp, :, mine], 19)

    for k in (5, 7, 6, 8):
        arrived(hr.at[0, 0], k)
    row_low = jnp.where(r > 0, 0.0, NEG)
    row_high = jnp.where(r < ROWS - 1, 0.0, NEG)

    def row_head(h, c):
        ln = pl.ds(pl.multiple_of(h * E, E), E)
        keys = jnp.concatenate([hr[0, 0, :, ln], k_ref[:, ln], hr[1, 0, :, ln], memk[:, ln]], axis=0)
        vals = jnp.concatenate([hr[0, 1, :, ln], v_ref[:, ln], hr[1, 1, :, ln], memv[:, ln]], axis=0)
        dq, dk, dv = unit(q_ref[:, ln], g_ref[:, ln], keys, vals, row_low, row_high)
        oq_ref[:, ln] = dq.astype(BF16)
        for a, d in enumerate((dk, dv)):
            gs[0, a, :, ln] = d[0:128].astype(BF16)
            own[a, :, ln] = d[128:256]
            gs[1, a, :, ln] = d[256:384].astype(BF16)
            dm[a, :, ln] = d[384:392]
        return c

    lax.fori_loop(0, 10, row_head, 0)

    for a in range(2):
        for s in range(S):
            ms2[a * S + s] = dm[a, s : s + 1, :]
    rs2[r] = ms2[r]
    push_all("row", in_row, ROWS, lambda t: ms2.at[t], rs2.at[r], 15)
    push(gs.at[0], gr.at[1], 11, {"row": before})
    push(gs.at[1], gr.at[0], 12, {"row": after})

    arrived(cgr.at[1], 13)
    arrived(cgr.at[0], 14)
    for a in range(2):
        full = jnp.concatenate(
            [
                cown[a, 0:128, :] + cgr[0, a].astype(F32),
                cown[a, 128:256, :] + cgr[1, a].astype(F32),
            ],
            axis=0,
        ).astype(BF16)
        bskv[:, a, :, :] = dot(from_stripe, full).astype(BF16).reshape(16, 16, PART)
    brkv[jp, :, :, mine] = bskv[r]
    push_all("row", in_row, ROWS, lambda t: bskv.at[t], brkv.at[jp, :, :, mine], 20)

    arrived(rs2.at[pl.ds(0, 15)], 15)
    to_the_block(jnp.sum(rs2[...], axis=0), zp2, zb2, 16)
    inside = to_the_blocks(zb2, bp2, bt2, 17, 20)
    to_the_row(inside, bt2, mp2, mem2, 18, 20, norm)

    from_pair = select_back(128, 128, by_pair)
    arrived(bsq.at[pl.ds(0, 15)], 19)

    def finish_q(h, c):
        ln = pl.ds(pl.multiple_of(h * 256, 256), 256)
        wide = pl.ds(pl.multiple_of(HALF + h * 256, 256), 256)
        oq_ref[:, wide] = dot(from_pair, brq[:, :, ln].reshape(128, 256)).astype(BF16)
        return c

    lax.fori_loop(0, 5, finish_q, 0)
    arrived(mem2.at[pl.ds(0, 15)], 18)
    for a in range(2):
        for s in range(S):
            dm[a, s : s + 1, :] = mem2[a * S + s]
    arrived(gr.at[1], 11)
    arrived(gr.at[0], 12)
    arrived(bskv.at[pl.ds(0, 15)], 20)

    def finish(h, c):
        ln = pl.ds(pl.multiple_of(h * 256, 256), 256)
        wide = pl.ds(pl.multiple_of(HALF + h * 256, 256), 256)
        for a, out in enumerate((ok_ref, ov_ref)):
            back = dot(from_pair, brkv[:, a, :, ln].reshape(128, 256))
            dr = dm[a, :, ln].astype(BF16)
            dc = dm[a, :, wide].astype(BF16)
            add_r = jnp.concatenate([dot(member_b[f], dr, 0, 0) for f in range(2)], axis=0)
            add_c = jnp.concatenate([dot(member_b[f], dc, 0, 0) for f in range(2)], axis=0)
            near = gr[0, a, :, ln].astype(F32) + gr[1, a, :, ln].astype(F32)
            out[:, ln] = (own[a, :, ln] + near + add_r).astype(BF16)
            out[:, wide] = (back + add_c).astype(BF16)
        return c

    lax.fori_loop(0, 5, finish, 0)

    left(ms.at[pl.ds(0, 15)], 0)
    left(zb.at[pl.ds(0, 7)], 1)
    left(bt.at[pl.ds(0, 3)], 2)
    left(mem.at[pl.ds(0, 15)], 3)
    left(crkv.at[pl.ds(0, 15)], 4)
    left(crqg.at[pl.ds(0, 15)], 21)
    for k in (5, 6, 7, 8):
        left(hr.at[0, 0], k)
    left(hc.at[1], 9)
    left(hc.at[0], 10)
    left(gs.at[0], 11)
    left(gs.at[1], 12)
    left(cgs.at[0], 13)
    left(cgs.at[1], 14)
    left(ms2.at[pl.ds(0, 15)], 15)
    left(zb2.at[pl.ds(0, 7)], 16)
    left(bt2.at[pl.ds(0, 3)], 17)
    left(mem2.at[pl.ds(0, 15)], 18)
    left(bsq.at[pl.ds(0, 15)], 19)
    left(bskv.at[pl.ds(0, 15)], 20)


def per_device(queries, keys, values, out_grad, slots, decay):
    flat = (TOKENS, FEATS)
    vm = pl.BlockSpec(memory_space=pltpu.VMEM)

    def row(count, width=FEATS):
        return pltpu.VMEM((count, 1, width), F32)

    scratch = [
        *[pltpu.VMEM(flat, BF16)] * 4, row(40),
        row(16, FEATS + 128), row(16, FEATS + 128),
        row(1), row(8), row(1), row(4), row(1), row(16),
        pltpu.VMEM((16, FEATS), BF16), pltpu.VMEM((16, FEATS), BF16),
        row(16), row(16),
        row(1), row(8), row(1), row(4), row(1), row(16),
        pltpu.VMEM((16, FEATS), F32), pltpu.VMEM((2, S, FEATS), F32),
        pltpu.VMEM((8, 2, 16, HALF), BF16),
        pltpu.VMEM((8, 2, 16, HALF), BF16),
        pltpu.VMEM((16, 2, 16, PART), BF16),
        pltpu.VMEM((16, 2, 16, PART), BF16),
        pltpu.VMEM((4, 2, 128, PART), BF16),
        pltpu.VMEM((2, 2, 128, HALF), BF16),
        pltpu.VMEM((2, 2, 128, PART), BF16),
        pltpu.VMEM((2, 2, 128, HALF), BF16),
        pltpu.VMEM((2, 2, 128, HALF), BF16),
        pltpu.VMEM((2, 128, HALF), F32),
        pltpu.VMEM((2, 256, PART), F32),
        pltpu.VMEM((2, 2, 128, PART), BF16),
        pltpu.VMEM((2, 2, 128, PART), BF16),
        pltpu.VMEM((16, 16, PART), BF16),
        pltpu.VMEM((16, 2, 16, PART), BF16),
        pltpu.VMEM((8, 16, HALF), BF16),
        pltpu.VMEM((8, 2, 16, HALF), BF16),
        pltpu.SemaphoreType.DMA((22,)),
        pltpu.SemaphoreType.DMA((22,)),
        pltpu.SemaphoreType.DMA((8,)),
    ]
    outs = pl.pallas_call(
        kernel,
        out_shape=[jax.ShapeDtypeStruct(flat, BF16)] * 3,
        in_specs=[pl.BlockSpec(memory_space=pltpu.HBM)] * 4 + [vm] + [pl.BlockSpec(memory_space=pltpu.SMEM)],
        out_specs=[vm] * 3,
        scratch_shapes=scratch,
        compiler_params=pltpu.CompilerParams(
            collective_id=0, has_side_effects=True, vmem_limit_bytes=48 * 1024 * 1024
        ),
    )(
        *[
            pltpu.with_memory_space_constraint(a.reshape(flat), pltpu.HBM)
            for a in (queries, keys, values, out_grad)
        ],
        slots, decay,
    )
    return tuple(o.reshape(queries.shape) for o in outs)


def solution(mesh):
    spec = P("group", "row", None, None)
    return jax.shard_map(
        per_device,
        mesh=mesh,
        in_specs=(spec, spec, spec, spec, P("group", "row", None), P()),
        out_specs=(spec, spec, spec),
        check_vma=False,
    )
```

```python
import jax
import jax.numpy as jnp
from jax import lax
from jax.experimental import pallas as pl
from jax.experimental.pallas import tpu as pltpu
from jax.sharding import PartitionSpec as P

S = 8
E = 128
TOKENS = 128
HALF = 1280
PART = 640
FEATS = 2560
ROWS = 16
MESH = pl.DeviceIdType.MESH
F32 = jnp.float32
BF16 = jnp.bfloat16
NEG = -1e30
STEPS = (
    (1, 0), (0, 1), (3, 0), (0, 3), (1, 1), (3, 3), (1, 3), (3, 1),
    (2, 0), (0, 2), (2, 1), (1, 2), (2, 3), (3, 2), (2, 2),
)
STEPS_X = sum(dx * 4**i for i, (dx, _) in enumerate(STEPS))
STEPS_Y = sum(dy * 4**i for i, (_, dy) in enumerate(STEPS))


def select(rows, cols, source):
    o = lax.broadcasted_iota(jnp.int32, (rows, cols), 0)
    i = lax.broadcasted_iota(jnp.int32, (rows, cols), 1)
    return jnp.where(source(o) == i, 1.0, 0.0).astype(BF16)


def select_back(rows, cols, source):
    i = lax.broadcasted_iota(jnp.int32, (rows, cols), 0)
    o = lax.broadcasted_iota(jnp.int32, (rows, cols), 1)
    return jnp.where(source(o) == i, 1.0, 0.0).astype(BF16)


def by_pair(s):
    return ((s >> 3) & 1) * 64 + (s >> 4) * 8 + (s & 7)


def by_stripe(o):
    return ((o >> 3) & 15) * 16 + ((o >> 2) & 1) * 8 + (o >> 7) * 4 + (o & 3)


def dot(a, b, ca=1, cb=0):
    return lax.dot_general(a, b, (((ca,), (cb,)), ((), ())), preferred_element_type=F32)


def unit(q, g, keys, values, low, high):
    scale = E ** (-0.5)
    s = dot(keys, q, 1, 1) * scale
    used = lax.broadcasted_iota(jnp.int32, (16, 128), 0) < S
    s = jnp.concatenate(
        [s[:128] + low, s[128:256], s[256:384] + high, jnp.where(used, s[384:], NEG)], axis=0
    )
    top = jnp.max(s, axis=0, keepdims=True)
    w = jnp.exp(s - top)
    p = w * (1.0 / jnp.sum(w, axis=0, keepdims=True))
    pb = p.astype(BF16)
    dprob = dot(values, g, 1, 1)
    delta = jnp.sum(pb.astype(F32) * dprob, axis=0, keepdims=True)
    ds = (p * ((dprob - delta) * scale)).astype(BF16)
    dk = dot(ds, q)
    dv = dot(pb, g)
    dq = dot(ds, keys, 0, 0)
    return dq, dk, dv


def kernel(
    qh_ref, kh_ref, vh_ref, gh_ref, slots_ref, decay_ref,
    oq_ref, ok_ref, ov_ref,
    q_ref, k_ref, v_ref, g_ref, wts,
    ms, rs, zp, zb, bp, bt, mp, mem, memk, memv,
    ms2, rs2, zp2, zb2, bp2, bt2, mp2, mem2,
    m2, dm,
    cskv, csqg, crkv, crqg, sep, hr, hc, gs, gr, own, cown, cgs, cgr,
    bsq, bskv, brq, brkv,
    send, recv, load,
):
    r = lax.axis_index("row")
    n = lax.axis_index("group")
    blk = n // 8
    idx = n % 8
    x = r // 4
    y = r % 4
    hh = y // 2
    yh = y % 2
    jp = x + yh * (7 - 2 * x)

    def holder(pair, part):
        high = pair // 4
        low = pair % 4
        return (low + high * (3 - 2 * low)) * 4 + part * 2 + high

    def in_row(d):
        return lax.rem(r + d, ROWS)

    def around(visit):
        def body(d, c):
            dx, dy = c
            visit(lax.rem(x + dx % 4, 4), lax.rem(y + dy % 4, 4))
            return dx // 4, dy // 4

        lax.fori_loop(0, len(STEPS), body, (jnp.int32(STEPS_X), jnp.int32(STEPS_Y)))

    def in_block(d):
        return blk * 8 + lax.rem(idx + d, 8)

    def in_blocks(d):
        return lax.rem(blk + d, 4) * 8 + idx

    barrier = pltpu.get_barrier_semaphore()

    def greet(axis, pick, count):
        def body(d, c):
            pl.semaphore_signal(barrier, inc=1, device_id={axis: pick(d)}, device_id_type=MESH)
            return c

        lax.fori_loop(1, count, body, 0)

    greet("row", in_row, ROWS)
    greet("group", in_block, 8)
    greet("group", in_blocks, 4)

    pairs = ((kh_ref, k_ref), (vh_ref, v_ref), (qh_ref, q_ref), (gh_ref, g_ref))

    def fetch(a, part):
        cols = (slice(None), pl.ds(part * HALF, HALF))
        return pltpu.make_async_copy(
            pairs[a][0].at[cols], pairs[a][1].at[cols], load.at[a * 2 + part]
        )

    for a in range(4):
        for part in (1, 0):
            fetch(a, part).start()

    def push(src, dst, k, device):
        pltpu.make_async_remote_copy(
            src_ref=src, dst_ref=dst, send_sem=send.at[k], recv_sem=recv.at[k],
            device_id=device, device_id_type=MESH,
        ).start()

    def arrived(shape_of, k):
        pltpu.make_async_copy(shape_of, shape_of, recv.at[k]).wait()

    def left(shape_of, k):
        pltpu.make_async_copy(shape_of, shape_of, send.at[k]).wait()

    def push_all(axis, pick, count, src, dst, k):
        def body(d, c):
            t = pick(d)
            push(src(t), dst, k, {axis: t})
            return c

        lax.fori_loop(1, count, body, 0)

    def push_row(src, dst, k):
        def visit(tx, ty):
            t = tx * 4 + ty
            push(src(t), dst, k, {"row": t})

        around(visit)

    to_pair = select(128, 128, by_pair)
    mine = pl.ds(pl.multiple_of(hh * PART, 128), PART)

    def arrange(first, second, to):
        def body(h, c):
            ln = pl.ds(pl.multiple_of(h * 256, 256), 256)
            wide = pl.ds(pl.multiple_of(HALF + h * 256, 256), 256)
            for a, ref in enumerate((first, second)):
                to[:, a, :, ln] = dot(to_pair, ref[:, wide]).astype(BF16).reshape(8, 16, 256)
            return c

        lax.fori_loop(0, 5, body, 0)

    for part in range(2):
        for a in range(2):
            fetch(a, part).wait()
    slot_iota = lax.broadcasted_iota(jnp.int32, (S, 64), 0)
    member = [jnp.where(slots_ref[f] == slot_iota, 1.0, 0.0) for f in range(2)]
    member_b = [m.astype(BF16) for m in member]
    count = jnp.sum(member[0] + member[1], axis=1, keepdims=True)
    for a, ref in enumerate((k_ref, v_ref)):
        total = dot(member_b[0], ref[0:64, :]) + dot(member_b[1], ref[64:128, :])
        for s in range(S):
            ms[a * S + s, :, 0:FEATS] = total[s : s + 1]
            ms[a * S + s, :, FEATS:] = jnp.broadcast_to(count[s : s + 1], (1, 128))
    rs[r] = ms[r]

    pl.semaphore_wait(barrier, 15 + 7 + 3)
    push_row(lambda t: ms.at[t], rs.at[r], 0)

    def scatter(source, to, k):
        def visit(tx, ty):
            tjp = tx + (ty % 2) * (7 - 2 * tx)
            lanes = pl.ds(pl.multiple_of((ty // 2) * PART, 128), PART)
            push(source.at[tjp, :, :, lanes], to.at[r], k, {"row": tx * 4 + ty})

        around(visit)

    arrange(k_ref, v_ref, cskv)
    scatter(cskv, crkv, 4)
    crkv[r] = cskv[jp, :, :, mine]
    fetch(2, 1).wait()
    fetch(3, 1).wait()
    arrange(q_ref, g_ref, csqg)
    scatter(csqg, crqg, 21)
    crqg[r] = csqg[jp, :, :, mine]

    log_rate = jnp.log(
        jnp.concatenate([jnp.full((1, 128), decay_ref[h], F32) for h in range(20)], axis=1)
    )

    def power(e):
        return jnp.exp(log_rate * e.astype(F32))

    for j in range(8):
        wts[j] = jnp.where(j < idx, power(idx - 1 - j), 0.0)
        wts[8 + j] = jnp.exp(log_rate * float(7 - j))
        wts[20 + j] = jnp.where(j > idx, power(j - idx - 1), 0.0)
        wts[28 + j] = jnp.exp(log_rate * float(j))
    for j in range(4):
        wts[16 + j] = jnp.where(j < blk, power(8 * (blk - 1 - j) + idx), 0.0)
        wts[36 + j] = jnp.where(j > blk, power(8 * (j - blk - 1) + 7 - idx), 0.0)

    fetch(2, 0).wait()
    fetch(3, 0).wait()

    def to_the_block(piece, zp_, zb_, k):
        zp_[0] = piece
        zb_[idx] = piece
        push_all("group", in_block, 8, lambda t: zp_.at[0], zb_.at[idx], k)

    def to_the_blocks(zb_, bp_, bt_, k, first):
        arrived(zb_.at[pl.ds(0, 7)], k - 1)
        whole = jnp.sum(zb_[...] * wts[first + 8 : first + 16], axis=0)
        bp_[0] = whole
        bt_[blk] = whole
        push_all("group", in_blocks, 4, lambda t: bp_.at[0], bt_.at[blk], k)
        return jnp.sum(zb_[...] * wts[first : first + 8], axis=0)

    def to_the_row(inside, bt_, mp_, mem_, k, first, norm_):
        arrived(bt_.at[pl.ds(0, 3)], k - 1)
        inside = inside + jnp.sum(bt_[...] * wts[first + 16 : first + 20], axis=0)
        if norm_ is not None:
            inside = inside * norm_
        mp_[0] = inside
        mem_[r] = inside
        push_row(lambda t: mp_.at[0], mem_.at[r], k)

    arrived(rs.at[pl.ds(0, 15)], 0)
    total = jnp.sum(rs[...], axis=0)
    norm = 1.0 / jnp.sqrt(jnp.maximum(total[:, FEATS : FEATS + 1], 1.0))
    to_the_block(total[:, :FEATS] * norm, zp, zb, 1)

    to_stripe = select(256, 256, by_stripe)

    def split(from_, a, to):
        block = from_[:, a, :, :].reshape(256, PART)
        sep[to] = dot(to_stripe, block).astype(BF16).reshape(2, 128, PART)

    pair_before = holder(lax.rem(jp + 7, 8), hh)
    pair_after = holder(lax.rem(jp + 1, 8), hh)
    arrived(crkv.at[pl.ds(0, 15)], 4)
    split(crkv, 0, 1)
    split(crkv, 1, 2)
    push(sep.at[pl.ds(1, 2), 0], hc.at[1], 9, {"row": pair_before})
    push(sep.at[pl.ds(1, 2), 1], hc.at[0], 10, {"row": pair_after})

    inside = to_the_blocks(zb, bp, bt, 2, 0)
    to_the_row(inside, bt, mp, mem, 3, 0, None)

    arrived(crqg.at[pl.ds(0, 15)], 21)
    before = lax.rem(r + ROWS - 1, ROWS)
    after = lax.rem(r + 1, ROWS)
    for i in range(2):
        cols = (slice(None), pl.ds(i * PART, PART))
        for a, ref in enumerate((k_ref, v_ref)):
            push(ref.at[cols], hr.at[i, 1, a], 22 + 4 * i + 2 * a, {"row": before})
            push(ref.at[cols], hr.at[i, 0, a], 23 + 4 * i + 2 * a, {"row": after})
    split(crqg, 0, 0)
    split(crqg, 1, 3)

    arrived(mem.at[pl.ds(0, 15)], 3)
    zero = jnp.zeros((S, FEATS), F32)
    m2[S:, :] = zero
    for a, to in enumerate((memk, memv)):
        for s in range(S):
            m2[s : s + 1, :] = mem[a * S + s]
        to[...] = m2[...].astype(BF16)
    dm[0] = zero
    dm[1] = zero

    arrived(hc.at[1], 9)
    arrived(hc.at[0], 10)
    col_low = jnp.where(jp > 0, 0.0, NEG)
    col_high = jnp.where(jp < 7, 0.0, NEG)

    def col_head(h, c):
        ln = pl.ds(pl.multiple_of(h * E, E), E)
        wide = pl.ds(pl.multiple_of(HALF + hh * PART + h * E, E), E)
        mk = memk[:, wide]
        mv = memv[:, wide]
        k0, k1, k2, k3 = hc[0, 0, :, ln], sep[1, 0, :, ln], sep[1, 1, :, ln], hc[1, 0, :, ln]
        v0, v1, v2, v3 = hc[0, 1, :, ln], sep[2, 0, :, ln], sep[2, 1, :, ln], hc[1, 1, :, ln]
        qa, ka, va = unit(
            sep[0, 0, :, ln], sep[3, 0, :, ln],
            jnp.concatenate([k0, k1, k2, mk], axis=0), jnp.concatenate([v0, v1, v2, mv], axis=0),
            col_low, 0.0,
        )
        qb, kb, vb = unit(
            sep[0, 1, :, ln], sep[3, 1, :, ln],
            jnp.concatenate([k1, k2, k3, mk], axis=0), jnp.concatenate([v1, v2, v3, mv], axis=0),
            0.0, col_high,
        )
        for a, (da, db) in enumerate(((ka, kb), (va, vb))):
            cgs[0, a, :, ln] = da[0:128].astype(BF16)
            cown[a, :, ln] = da[128:384] + db[0:256]
            cgs[1, a, :, ln] = db[256:384].astype(BF16)
            dm[a, :, wide] = da[384:392] + db[384:392]
        sep[0, 0, :, ln] = qa.astype(BF16)
        sep[0, 1, :, ln] = qb.astype(BF16)
        return c

    lax.fori_loop(0, 5, col_head, 0)
    push(cgs.at[0], cgr.at[1], 13, {"row": pair_before})
    push(cgs.at[1], cgr.at[0], 14, {"row": pair_after})
    from_stripe = select_back(256, 256, by_stripe)
    bsq[...] = dot(from_stripe, sep[0].reshape(256, PART)).astype(BF16).reshape(16, 16, PART)
    brq[jp, :, mine] = bsq[r]
    push_row(lambda t: bsq.at[t], brq.at[jp, :, mine], 19)

    row_low = jnp.where(r > 0, 0.0, NEG)
    row_high = jnp.where(r < ROWS - 1, 0.0, NEG)

    def row_heads(i):
        for k in range(4):
            arrived(hr.at[0, 0, 0], 22 + 4 * i + k)

        def body(h, c):
            near = pl.ds(pl.multiple_of(h * E, E), E)
            ln = pl.ds(pl.multiple_of(i * PART + h * E, E), E)
            keys = jnp.concatenate(
                [hr[i, 0, 0, :, near], k_ref[:, ln], hr[i, 1, 0, :, near], memk[:, ln]], axis=0
            )
            vals = jnp.concatenate(
                [hr[i, 0, 1, :, near], v_ref[:, ln], hr[i, 1, 1, :, near], memv[:, ln]], axis=0
            )
            dq, dk, dv = unit(q_ref[:, ln], g_ref[:, ln], keys, vals, row_low, row_high)
            oq_ref[:, ln] = dq.astype(BF16)
            for a, d in enumerate((dk, dv)):
                gs[i, 0, a, :, near] = d[0:128].astype(BF16)
                own[a, :, ln] = d[128:256]
                gs[i, 1, a, :, near] = d[256:384].astype(BF16)
                dm[a, :, ln] = d[384:392]
            return c

        lax.fori_loop(0, 5, body, 0)

    def row_back(i):
        push(gs.at[i, 0], gr.at[i, 1], 5 + 2 * i, {"row": before})
        push(gs.at[i, 1], gr.at[i, 0], 6 + 2 * i, {"row": after})

    row_heads(0)
    row_back(0)
    row_heads(1)

    for a in range(2):
        for s in range(S):
            ms2[a * S + s] = dm[a, s : s + 1, :]
    rs2[r] = ms2[r]
    push_row(lambda t: ms2.at[t], rs2.at[r], 15)
    row_back(1)

    arrived(cgr.at[1], 13)
    arrived(cgr.at[0], 14)
    for a in range(2):
        full = jnp.concatenate(
            [
                cown[a, 0:128, :] + cgr[0, a].astype(F32),
                cown[a, 128:256, :] + cgr[1, a].astype(F32),
            ],
            axis=0,
        ).astype(BF16)
        bskv[:, a, :, :] = dot(from_stripe, full).astype(BF16).reshape(16, 16, PART)
    brkv[jp, :, :, mine] = bskv[r]
    push_row(lambda t: bskv.at[t], brkv.at[jp, :, :, mine], 20)

    arrived(rs2.at[pl.ds(0, 15)], 15)
    to_the_block(jnp.sum(rs2[...], axis=0), zp2, zb2, 16)
    inside = to_the_blocks(zb2, bp2, bt2, 17, 20)
    to_the_row(inside, bt2, mp2, mem2, 18, 20, norm)

    from_pair = select_back(128, 128, by_pair)
    arrived(bsq.at[pl.ds(0, 15)], 19)

    def finish_q(h, c):
        ln = pl.ds(pl.multiple_of(h * 256, 256), 256)
        wide = pl.ds(pl.multiple_of(HALF + h * 256, 256), 256)
        oq_ref[:, wide] = dot(from_pair, brq[:, :, ln].reshape(128, 256)).astype(BF16)
        return c

    lax.fori_loop(0, 5, finish_q, 0)
    for i in range(2):
        cols = pl.ds(i * PART, PART)
        arrived(gr.at[i, 0], 5 + 2 * i)
        arrived(gr.at[i, 1], 6 + 2 * i)
        for a in range(2):
            own[a, :, cols] = (
                own[a, :, cols] + gr[i, 0, a].astype(F32) + gr[i, 1, a].astype(F32)
            )
    arrived(mem2.at[pl.ds(0, 15)], 18)
    for a in range(2):
        for s in range(S):
            dm[a, s : s + 1, :] = mem2[a * S + s]
    arrived(bskv.at[pl.ds(0, 15)], 20)

    def finish(h, c):
        ln = pl.ds(pl.multiple_of(h * 256, 256), 256)
        wide = pl.ds(pl.multiple_of(HALF + h * 256, 256), 256)
        for a, out in enumerate((ok_ref, ov_ref)):
            back = dot(from_pair, brkv[:, a, :, ln].reshape(128, 256))
            dr = dm[a, :, ln].astype(BF16)
            dc = dm[a, :, wide].astype(BF16)
            add_r = jnp.concatenate([dot(member_b[f], dr, 0, 0) for f in range(2)], axis=0)
            add_c = jnp.concatenate([dot(member_b[f], dc, 0, 0) for f in range(2)], axis=0)
            out[:, ln] = (own[a, :, ln] + add_r).astype(BF16)
            out[:, wide] = (back + add_c).astype(BF16)
        return c

    lax.fori_loop(0, 5, finish, 0)

    left(ms.at[pl.ds(0, 15)], 0)
    left(zb.at[pl.ds(0, 7)], 1)
    left(bt.at[pl.ds(0, 3)], 2)
    left(mem.at[pl.ds(0, 15)], 3)
    left(crkv.at[pl.ds(0, 15)], 4)
    left(crqg.at[pl.ds(0, 15)], 21)
    for k in range(8):
        left(hr.at[0, 0, 0], 22 + k)
    for k in range(4):
        left(gs.at[0, 0], 5 + k)
    left(hc.at[1], 9)
    left(hc.at[0], 10)
    left(cgs.at[0], 13)
    left(cgs.at[1], 14)
    left(ms2.at[pl.ds(0, 15)], 15)
    left(zb2.at[pl.ds(0, 7)], 16)
    left(bt2.at[pl.ds(0, 3)], 17)
    left(mem2.at[pl.ds(0, 15)], 18)
    left(bsq.at[pl.ds(0, 15)], 19)
    left(bskv.at[pl.ds(0, 15)], 20)


def per_device(queries, keys, values, out_grad, slots, decay):
    flat = (TOKENS, FEATS)
    vm = pl.BlockSpec(memory_space=pltpu.VMEM)

    def row(count, width=FEATS):
        return pltpu.VMEM((count, 1, width), F32)

    scratch = [
        *[pltpu.VMEM(flat, BF16)] * 4, row(40),
        row(16, FEATS + 128), row(16, FEATS + 128),
        row(1), row(8), row(1), row(4), row(1), row(16),
        pltpu.VMEM((16, FEATS), BF16), pltpu.VMEM((16, FEATS), BF16),
        row(16), row(16),
        row(1), row(8), row(1), row(4), row(1), row(16),
        pltpu.VMEM((16, FEATS), F32), pltpu.VMEM((2, S, FEATS), F32),
        pltpu.VMEM((8, 2, 16, HALF), BF16),
        pltpu.VMEM((8, 2, 16, HALF), BF16),
        pltpu.VMEM((16, 2, 16, PART), BF16),
        pltpu.VMEM((16, 2, 16, PART), BF16),
        pltpu.VMEM((4, 2, 128, PART), BF16),
        pltpu.VMEM((2, 2, 2, 128, PART), BF16),
        pltpu.VMEM((2, 2, 128, PART), BF16),
        pltpu.VMEM((2, 2, 2, 128, PART), BF16),
        pltpu.VMEM((2, 2, 2, 128, PART), BF16),
        pltpu.VMEM((2, 128, HALF), F32),
        pltpu.VMEM((2, 256, PART), F32),
        pltpu.VMEM((2, 2, 128, PART), BF16),
        pltpu.VMEM((2, 2, 128, PART), BF16),
        pltpu.VMEM((16, 16, PART), BF16),
        pltpu.VMEM((16, 2, 16, PART), BF16),
        pltpu.VMEM((8, 16, HALF), BF16),
        pltpu.VMEM((8, 2, 16, HALF), BF16),
        pltpu.SemaphoreType.DMA((30,)),
        pltpu.SemaphoreType.DMA((30,)),
        pltpu.SemaphoreType.DMA((8,)),
    ]
    outs = pl.pallas_call(
        kernel,
        out_shape=[jax.ShapeDtypeStruct(flat, BF16)] * 3,
        in_specs=[pl.BlockSpec(memory_space=pltpu.HBM)] * 4 + [vm] + [pl.BlockSpec(memory_space=pltpu.SMEM)],
        out_specs=[vm] * 3,
        scratch_shapes=scratch,
        compiler_params=pltpu.CompilerParams(
            collective_id=0, has_side_effects=True, vmem_limit_bytes=48 * 1024 * 1024
        ),
    )(
        *[
            pltpu.with_memory_space_constraint(a.reshape(flat), pltpu.HBM)
            for a in (queries, keys, values, out_grad)
        ],
        slots, decay,
    )
    return tuple(o.reshape(queries.shape) for o in outs)


def solution(mesh):
    spec = P("group", "row", None, None)
    return jax.shard_map(
        per_device,
        mesh=mesh,
        in_specs=(spec, spec, spec, spec, P("group", "row", None), P()),
        out_specs=(spec, spec, spec),
        check_vma=False,
    )
```

```python
import jax
import jax.numpy as jnp
from jax import lax
from jax.experimental import pallas as pl
from jax.experimental.pallas import tpu as pltpu
from jax.sharding import PartitionSpec as P

S = 8
E = 128
TOKENS = 128
HALF = 1280
PART = 640
FEATS = 2560
ROWS = 16
MESH = pl.DeviceIdType.MESH
F32 = jnp.float32
BF16 = jnp.bfloat16
NEG = -1e30
STEPS = (
    (1, 0), (0, 1), (3, 0), (0, 3), (1, 1), (3, 3), (1, 3), (3, 1),
    (2, 0), (0, 2), (2, 1), (1, 2), (2, 3), (3, 2), (2, 2),
)
STEPS_X = sum(dx * 4**i for i, (dx, _) in enumerate(STEPS))
STEPS_Y = sum(dy * 4**i for i, (_, dy) in enumerate(STEPS))


def select(rows, cols, source):
    o = lax.broadcasted_iota(jnp.int32, (rows, cols), 0)
    i = lax.broadcasted_iota(jnp.int32, (rows, cols), 1)
    return jnp.where(source(o) == i, 1.0, 0.0).astype(BF16)


def select_back(rows, cols, source):
    i = lax.broadcasted_iota(jnp.int32, (rows, cols), 0)
    o = lax.broadcasted_iota(jnp.int32, (rows, cols), 1)
    return jnp.where(source(o) == i, 1.0, 0.0).astype(BF16)


def by_pair(s):
    return ((s >> 3) & 1) * 64 + (s >> 4) * 8 + (s & 7)


def by_stripe(o):
    return ((o >> 3) & 15) * 16 + ((o >> 2) & 1) * 8 + (o >> 7) * 4 + (o & 3)


def dot(a, b, ca=1, cb=0):
    return lax.dot_general(a, b, (((ca,), (cb,)), ((), ())), preferred_element_type=F32)


def unit(q, g, keys, values, low, high):
    scale = E ** (-0.5)
    s = dot(keys, q, 1, 1) * scale
    used = lax.broadcasted_iota(jnp.int32, (16, 128), 0) < S
    s = jnp.concatenate(
        [s[:128] + low, s[128:256], s[256:384] + high, jnp.where(used, s[384:], NEG)], axis=0
    )
    top = jnp.max(s, axis=0, keepdims=True)
    w = jnp.exp(s - top)
    p = w * (1.0 / jnp.sum(w, axis=0, keepdims=True))
    pb = p.astype(BF16)
    dprob = dot(values, g, 1, 1)
    delta = jnp.sum(pb.astype(F32) * dprob, axis=0, keepdims=True)
    ds = (p * ((dprob - delta) * scale)).astype(BF16)
    dk = dot(ds, q)
    dv = dot(pb, g)
    dq = dot(ds, keys, 0, 0)
    return dq, dk, dv


def kernel(
    qh_ref, kh_ref, vh_ref, gh_ref, slots_ref, decay_ref,
    oq_ref, ok_ref, ov_ref,
    q_ref, k_ref, v_ref, g_ref, wts,
    ms, rs, zp, zb, bp, bt, mp, mem, memk, memv,
    ms2, rs2, zp2, zb2, bp2, bt2, mp2, mem2,
    m2, dm,
    cskv, csq, csg, crkv, crq, crg, sep, hr, hc, gs, gr, own, cown, cgs, cgr,
    bsq, bsk, bsv, brq, brk, brv,
    send, recv, load,
):
    r = lax.axis_index("row")
    n = lax.axis_index("group")
    blk = n // 8
    idx = n % 8
    x = r // 4
    y = r % 4
    hh = y // 2
    yh = y % 2
    jp = x + yh * (7 - 2 * x)

    def holder(pair, part):
        high = pair // 4
        low = pair % 4
        return (low + high * (3 - 2 * low)) * 4 + part * 2 + high

    def in_row(d):
        return lax.rem(r + d, ROWS)

    def around(visit):
        def body(d, c):
            dx, dy = c
            visit(lax.rem(x + dx % 4, 4), lax.rem(y + dy % 4, 4))
            return dx // 4, dy // 4

        lax.fori_loop(0, len(STEPS), body, (jnp.int32(STEPS_X), jnp.int32(STEPS_Y)))

    def in_block(d):
        return blk * 8 + lax.rem(idx + d, 8)

    def in_blocks(d):
        return lax.rem(blk + d, 4) * 8 + idx

    barrier = pltpu.get_barrier_semaphore()

    def greet(axis, pick, count):
        def body(d, c):
            pl.semaphore_signal(barrier, inc=1, device_id={axis: pick(d)}, device_id_type=MESH)
            return c

        lax.fori_loop(1, count, body, 0)

    greet("row", in_row, ROWS)
    greet("group", in_block, 8)
    greet("group", in_blocks, 4)

    pairs = ((kh_ref, k_ref), (vh_ref, v_ref), (qh_ref, q_ref), (gh_ref, g_ref))

    def fetch(a, part):
        cols = (slice(None), pl.ds(part * HALF, HALF))
        return pltpu.make_async_copy(
            pairs[a][0].at[cols], pairs[a][1].at[cols], load.at[a * 2 + part]
        )

    for a in range(4):
        for part in (1, 0):
            fetch(a, part).start()

    def push(src, dst, k, device):
        pltpu.make_async_remote_copy(
            src_ref=src, dst_ref=dst, send_sem=send.at[k], recv_sem=recv.at[k],
            device_id=device, device_id_type=MESH,
        ).start()

    def arrived(shape_of, k):
        pltpu.make_async_copy(shape_of, shape_of, recv.at[k]).wait()

    def left(shape_of, k):
        pltpu.make_async_copy(shape_of, shape_of, send.at[k]).wait()

    def push_all(axis, pick, count, src, dst, k):
        def body(d, c):
            t = pick(d)
            push(src(t), dst, k, {axis: t})
            return c

        lax.fori_loop(1, count, body, 0)

    def push_row(src, dst, k):
        def visit(tx, ty):
            t = tx * 4 + ty
            push(src(t), dst, k, {"row": t})

        around(visit)

    to_pair = select(128, 128, by_pair)
    mine = pl.ds(pl.multiple_of(hh * PART, 128), PART)

    def arrange(refs, to):
        def body(h, c):
            ln = pl.ds(pl.multiple_of(h * 256, 256), 256)
            wide = pl.ds(pl.multiple_of(HALF + h * 256, 256), 256)
            for a, ref in enumerate(refs):
                to[:, a, :, ln] = dot(to_pair, ref[:, wide]).astype(BF16).reshape(8, 16, 256)
            return c

        lax.fori_loop(0, 5, body, 0)

    for part in range(2):
        for a in range(2):
            fetch(a, part).wait()
    slot_iota = lax.broadcasted_iota(jnp.int32, (S, 64), 0)
    member = [jnp.where(slots_ref[f] == slot_iota, 1.0, 0.0) for f in range(2)]
    member_b = [m.astype(BF16) for m in member]
    count = jnp.sum(member[0] + member[1], axis=1, keepdims=True)
    for a, ref in enumerate((k_ref, v_ref)):
        total = dot(member_b[0], ref[0:64, :]) + dot(member_b[1], ref[64:128, :])
        for s in range(S):
            ms[a * S + s, :, 0:FEATS] = total[s : s + 1]
            ms[a * S + s, :, FEATS:] = jnp.broadcast_to(count[s : s + 1], (1, 128))
    rs[r] = ms[r]

    pl.semaphore_wait(barrier, 15 + 7 + 3)
    push_row(lambda t: ms.at[t], rs.at[r], 0)

    def scatter(source, to, k):
        def visit(tx, ty):
            tjp = tx + (ty % 2) * (7 - 2 * tx)
            lanes = pl.ds(pl.multiple_of((ty // 2) * PART, 128), PART)
            push(source.at[tjp, :, :, lanes], to.at[r], k, {"row": tx * 4 + ty})

        around(visit)

    arrange((k_ref, v_ref), cskv)
    scatter(cskv, crkv, 4)
    crkv[r] = cskv[jp, :, :, mine]
    for a, ref, cut, to in ((2, q_ref, csq, crq), (3, g_ref, csg, crg)):
        fetch(a, 1).wait()
        arrange((ref,), cut)
        to[r] = cut[jp, :, :, mine]

    log_rate = jnp.log(
        jnp.concatenate([jnp.full((1, 128), decay_ref[h], F32) for h in range(20)], axis=1)
    )

    def power(e):
        return jnp.exp(log_rate * e.astype(F32))

    for j in range(8):
        wts[j] = jnp.where(j < idx, power(idx - 1 - j), 0.0)
        wts[8 + j] = jnp.exp(log_rate * float(7 - j))
        wts[20 + j] = jnp.where(j > idx, power(j - idx - 1), 0.0)
        wts[28 + j] = jnp.exp(log_rate * float(j))
    for j in range(4):
        wts[16 + j] = jnp.where(j < blk, power(8 * (blk - 1 - j) + idx), 0.0)
        wts[36 + j] = jnp.where(j > blk, power(8 * (j - blk - 1) + 7 - idx), 0.0)

    fetch(2, 0).wait()
    fetch(3, 0).wait()

    def to_the_block(piece, zp_, zb_, k):
        zp_[0] = piece
        zb_[idx] = piece
        push_all("group", in_block, 8, lambda t: zp_.at[0], zb_.at[idx], k)

    def to_the_blocks(zb_, bp_, bt_, k, first):
        arrived(zb_.at[pl.ds(0, 7)], k - 1)
        whole = jnp.sum(zb_[...] * wts[first + 8 : first + 16], axis=0)
        bp_[0] = whole
        bt_[blk] = whole
        push_all("group", in_blocks, 4, lambda t: bp_.at[0], bt_.at[blk], k)
        return jnp.sum(zb_[...] * wts[first : first + 8], axis=0)

    def to_the_row(inside, bt_, mp_, mem_, k, first, norm_):
        arrived(bt_.at[pl.ds(0, 3)], k - 1)
        inside = inside + jnp.sum(bt_[...] * wts[first + 16 : first + 20], axis=0)
        if norm_ is not None:
            inside = inside * norm_
        mp_[0] = inside
        mem_[r] = inside
        push_row(lambda t: mp_.at[0], mem_.at[r], k)

    arrived(rs.at[pl.ds(0, 15)], 0)
    total = jnp.sum(rs[...], axis=0)
    norm = 1.0 / jnp.sqrt(jnp.maximum(total[:, FEATS : FEATS + 1], 1.0))
    to_the_block(total[:, :FEATS] * norm, zp, zb, 1)
    scatter(csq, crq, 21)

    to_stripe = select(256, 256, by_stripe)

    def split(from_, a, to):
        block = from_[:, a, :, :].reshape(256, PART)
        sep[to] = dot(to_stripe, block).astype(BF16).reshape(2, 128, PART)

    pair_before = holder(lax.rem(jp + 7, 8), hh)
    pair_after = holder(lax.rem(jp + 1, 8), hh)
    arrived(crkv.at[pl.ds(0, 15)], 4)
    split(crkv, 0, 1)
    split(crkv, 1, 2)
    inside = to_the_blocks(zb, bp, bt, 2, 0)
    push(sep.at[pl.ds(1, 2), 0], hc.at[1], 9, {"row": pair_before})
    push(sep.at[pl.ds(1, 2), 1], hc.at[0], 10, {"row": pair_after})
    scatter(csg, crg, 12)
    to_the_row(inside, bt, mp, mem, 3, 0, None)

    before = lax.rem(r + ROWS - 1, ROWS)
    after = lax.rem(r + 1, ROWS)
    for i in range(2):
        cols = (slice(None), pl.ds(i * PART, PART))
        for a, ref in enumerate((k_ref, v_ref)):
            push(ref.at[cols], hr.at[i, 1, a], 22 + 4 * i + 2 * a, {"row": before})
            push(ref.at[cols], hr.at[i, 0, a], 23 + 4 * i + 2 * a, {"row": after})
    arrived(crq.at[pl.ds(0, 15)], 21)
    split(crq, 0, 0)
    arrived(crg.at[pl.ds(0, 15)], 12)
    split(crg, 0, 3)

    arrived(mem.at[pl.ds(0, 15)], 3)
    zero = jnp.zeros((S, FEATS), F32)
    m2[S:, :] = zero
    for a, to in enumerate((memk, memv)):
        for s in range(S):
            m2[s : s + 1, :] = mem[a * S + s]
        to[...] = m2[...].astype(BF16)
    dm[0] = zero
    dm[1] = zero

    arrived(hc.at[1], 9)
    arrived(hc.at[0], 10)
    col_low = jnp.where(jp > 0, 0.0, NEG)
    col_high = jnp.where(jp < 7, 0.0, NEG)

    def col_head(h, c):
        ln = pl.ds(pl.multiple_of(h * E, E), E)
        wide = pl.ds(pl.multiple_of(HALF + hh * PART + h * E, E), E)
        mk = memk[:, wide]
        mv = memv[:, wide]
        k0, k1, k2, k3 = hc[0, 0, :, ln], sep[1, 0, :, ln], sep[1, 1, :, ln], hc[1, 0, :, ln]
        v0, v1, v2, v3 = hc[0, 1, :, ln], sep[2, 0, :, ln], sep[2, 1, :, ln], hc[1, 1, :, ln]
        qa, ka, va = unit(
            sep[0, 0, :, ln], sep[3, 0, :, ln],
            jnp.concatenate([k0, k1, k2, mk], axis=0), jnp.concatenate([v0, v1, v2, mv], axis=0),
            col_low, 0.0,
        )
        qb, kb, vb = unit(
            sep[0, 1, :, ln], sep[3, 1, :, ln],
            jnp.concatenate([k1, k2, k3, mk], axis=0), jnp.concatenate([v1, v2, v3, mv], axis=0),
            0.0, col_high,
        )
        for a, (da, db) in enumerate(((ka, kb), (va, vb))):
            cgs[0, a, :, ln] = da[0:128].astype(BF16)
            cown[a, :, ln] = da[128:384] + db[0:256]
            cgs[1, a, :, ln] = db[256:384].astype(BF16)
            dm[a, :, wide] = da[384:392] + db[384:392]
        sep[0, 0, :, ln] = qa.astype(BF16)
        sep[0, 1, :, ln] = qb.astype(BF16)
        return c

    lax.fori_loop(0, 5, col_head, 0)
    push(cgs.at[0], cgr.at[1], 13, {"row": pair_before})
    push(cgs.at[1], cgr.at[0], 14, {"row": pair_after})
    from_stripe = select_back(256, 256, by_stripe)
    bsq[...] = dot(from_stripe, sep[0].reshape(256, PART)).astype(BF16).reshape(16, 16, PART)
    brq[jp, :, mine] = bsq[r]
    push_row(lambda t: bsq.at[t], brq.at[jp, :, mine], 19)

    row_low = jnp.where(r > 0, 0.0, NEG)
    row_high = jnp.where(r < ROWS - 1, 0.0, NEG)

    def row_heads(i):
        for k in range(4):
            arrived(hr.at[0, 0, 0], 22 + 4 * i + k)

        def body(h, c):
            near = pl.ds(pl.multiple_of(h * E, E), E)
            ln = pl.ds(pl.multiple_of(i * PART + h * E, E), E)
            keys = jnp.concatenate(
                [hr[i, 0, 0, :, near], k_ref[:, ln], hr[i, 1, 0, :, near], memk[:, ln]], axis=0
            )
            vals = jnp.concatenate(
                [hr[i, 0, 1, :, near], v_ref[:, ln], hr[i, 1, 1, :, near], memv[:, ln]], axis=0
            )
            dq, dk, dv = unit(q_ref[:, ln], g_ref[:, ln], keys, vals, row_low, row_high)
            oq_ref[:, ln] = dq.astype(BF16)
            for a, d in enumerate((dk, dv)):
                gs[i, 0, a, :, near] = d[0:128].astype(BF16)
                own[a, :, ln] = d[128:256]
                gs[i, 1, a, :, near] = d[256:384].astype(BF16)
                dm[a, :, ln] = d[384:392]
            return c

        lax.fori_loop(0, 5, body, 0)

    def row_back(i):
        push(gs.at[i, 0], gr.at[i, 1], 5 + 2 * i, {"row": before})
        push(gs.at[i, 1], gr.at[i, 0], 6 + 2 * i, {"row": after})

    row_heads(0)
    row_heads(1)

    for a in range(2):
        for s in range(S):
            ms2[a * S + s] = dm[a, s : s + 1, :]
    rs2[r] = ms2[r]
    push_row(lambda t: ms2.at[t], rs2.at[r], 15)
    row_back(0)

    arrived(cgr.at[1], 13)
    arrived(cgr.at[0], 14)
    for a, (cut, to) in enumerate(((bsk, brk), (bsv, brv))):
        full = jnp.concatenate(
            [
                cown[a, 0:128, :] + cgr[0, a].astype(F32),
                cown[a, 128:256, :] + cgr[1, a].astype(F32),
            ],
            axis=0,
        ).astype(BF16)
        cut[...] = dot(from_stripe, full).astype(BF16).reshape(16, 16, PART)
        to[jp, :, mine] = cut[r]

    arrived(rs2.at[pl.ds(0, 15)], 15)
    to_the_block(jnp.sum(rs2[...], axis=0), zp2, zb2, 16)
    push_row(lambda t: bsk.at[t], brk.at[jp, :, mine], 20)
    inside = to_the_blocks(zb2, bp2, bt2, 17, 20)
    push_row(lambda t: bsv.at[t], brv.at[jp, :, mine], 11)
    to_the_row(inside, bt2, mp2, mem2, 18, 20, norm)
    row_back(1)

    from_pair = select_back(128, 128, by_pair)
    arrived(bsq.at[pl.ds(0, 15)], 19)

    def finish_q(h, c):
        ln = pl.ds(pl.multiple_of(h * 256, 256), 256)
        wide = pl.ds(pl.multiple_of(HALF + h * 256, 256), 256)
        oq_ref[:, wide] = dot(from_pair, brq[:, :, ln].reshape(128, 256)).astype(BF16)
        return c

    lax.fori_loop(0, 5, finish_q, 0)
    for i in range(2):
        cols = pl.ds(i * PART, PART)
        arrived(gr.at[i, 0], 5 + 2 * i)
        arrived(gr.at[i, 1], 6 + 2 * i)
        for a in range(2):
            own[a, :, cols] = (
                own[a, :, cols] + gr[i, 0, a].astype(F32) + gr[i, 1, a].astype(F32)
            )
    arrived(mem2.at[pl.ds(0, 15)], 18)
    for a in range(2):
        for s in range(S):
            dm[a, s : s + 1, :] = mem2[a * S + s]
    arrived(bsk.at[pl.ds(0, 15)], 20)
    arrived(bsv.at[pl.ds(0, 15)], 11)

    def finish(h, c):
        ln = pl.ds(pl.multiple_of(h * 256, 256), 256)
        wide = pl.ds(pl.multiple_of(HALF + h * 256, 256), 256)
        for a, (from_, out) in enumerate(((brk, ok_ref), (brv, ov_ref))):
            back = dot(from_pair, from_[:, :, ln].reshape(128, 256))
            dr = dm[a, :, ln].astype(BF16)
            dc = dm[a, :, wide].astype(BF16)
            add_r = jnp.concatenate([dot(member_b[f], dr, 0, 0) for f in range(2)], axis=0)
            add_c = jnp.concatenate([dot(member_b[f], dc, 0, 0) for f in range(2)], axis=0)
            out[:, ln] = (own[a, :, ln] + add_r).astype(BF16)
            out[:, wide] = (back + add_c).astype(BF16)
        return c

    lax.fori_loop(0, 5, finish, 0)

    left(ms.at[pl.ds(0, 15)], 0)
    left(zb.at[pl.ds(0, 7)], 1)
    left(bt.at[pl.ds(0, 3)], 2)
    left(mem.at[pl.ds(0, 15)], 3)
    left(crkv.at[pl.ds(0, 15)], 4)
    left(crq.at[pl.ds(0, 15)], 21)
    left(crg.at[pl.ds(0, 15)], 12)
    for k in range(8):
        left(hr.at[0, 0, 0], 22 + k)
    for k in range(4):
        left(gs.at[0, 0], 5 + k)
    left(hc.at[1], 9)
    left(hc.at[0], 10)
    left(cgs.at[0], 13)
    left(cgs.at[1], 14)
    left(ms2.at[pl.ds(0, 15)], 15)
    left(zb2.at[pl.ds(0, 7)], 16)
    left(bt2.at[pl.ds(0, 3)], 17)
    left(mem2.at[pl.ds(0, 15)], 18)
    left(bsq.at[pl.ds(0, 15)], 19)
    left(bsk.at[pl.ds(0, 15)], 20)
    left(bsv.at[pl.ds(0, 15)], 11)


def per_device(queries, keys, values, out_grad, slots, decay):
    flat = (TOKENS, FEATS)
    vm = pl.BlockSpec(memory_space=pltpu.VMEM)

    def row(count, width=FEATS):
        return pltpu.VMEM((count, 1, width), F32)

    scratch = [
        *[pltpu.VMEM(flat, BF16)] * 4, row(40),
        row(16, FEATS + 128), row(16, FEATS + 128),
        row(1), row(8), row(1), row(4), row(1), row(16),
        pltpu.VMEM((16, FEATS), BF16), pltpu.VMEM((16, FEATS), BF16),
        row(16), row(16),
        row(1), row(8), row(1), row(4), row(1), row(16),
        pltpu.VMEM((16, FEATS), F32), pltpu.VMEM((2, S, FEATS), F32),
        pltpu.VMEM((8, 2, 16, HALF), BF16),
        pltpu.VMEM((8, 1, 16, HALF), BF16),
        pltpu.VMEM((8, 1, 16, HALF), BF16),
        pltpu.VMEM((16, 2, 16, PART), BF16),
        pltpu.VMEM((16, 1, 16, PART), BF16),
        pltpu.VMEM((16, 1, 16, PART), BF16),
        pltpu.VMEM((4, 2, 128, PART), BF16),
        pltpu.VMEM((2, 2, 2, 128, PART), BF16),
        pltpu.VMEM((2, 2, 128, PART), BF16),
        pltpu.VMEM((2, 2, 2, 128, PART), BF16),
        pltpu.VMEM((2, 2, 2, 128, PART), BF16),
        pltpu.VMEM((2, 128, HALF), F32),
        pltpu.VMEM((2, 256, PART), F32),
        pltpu.VMEM((2, 2, 128, PART), BF16),
        pltpu.VMEM((2, 2, 128, PART), BF16),
        *[pltpu.VMEM((16, 16, PART), BF16)] * 3,
        *[pltpu.VMEM((8, 16, HALF), BF16)] * 3,
        pltpu.SemaphoreType.DMA((30,)),
        pltpu.SemaphoreType.DMA((30,)),
        pltpu.SemaphoreType.DMA((8,)),
    ]
    outs = pl.pallas_call(
        kernel,
        out_shape=[jax.ShapeDtypeStruct(flat, BF16)] * 3,
        in_specs=[pl.BlockSpec(memory_space=pltpu.HBM)] * 4 + [vm] + [pl.BlockSpec(memory_space=pltpu.SMEM)],
        out_specs=[vm] * 3,
        scratch_shapes=scratch,
        compiler_params=pltpu.CompilerParams(
            collective_id=0, has_side_effects=True, vmem_limit_bytes=48 * 1024 * 1024
        ),
    )(
        *[
            pltpu.with_memory_space_constraint(a.reshape(flat), pltpu.HBM)
            for a in (queries, keys, values, out_grad)
        ],
        slots, decay,
    )
    return tuple(o.reshape(queries.shape) for o in outs)


def solution(mesh):
    spec = P("group", "row", None, None)
    return jax.shard_map(
        per_device,
        mesh=mesh,
        in_specs=(spec, spec, spec, spec, P("group", "row", None), P()),
        out_specs=(spec, spec, spec),
        check_vma=False,
    )
```

```python
import jax
import jax.numpy as jnp
from jax import lax
from jax.experimental import pallas as pl
from jax.experimental.pallas import tpu as pltpu
from jax.sharding import PartitionSpec as P

S = 8
E = 128
TOKENS = 128
HALF = 1280
PART = 640
FEATS = 2560
ROWS = 16
MESH = pl.DeviceIdType.MESH
F32 = jnp.float32
BF16 = jnp.bfloat16
NEG = -1e30
STEPS = (
    (1, 0), (0, 1), (3, 0), (0, 3), (1, 1), (3, 3), (1, 3), (3, 1),
    (2, 0), (0, 2), (2, 1), (1, 2), (2, 3), (3, 2), (2, 2),
)
STEPS_X = sum(dx * 4**i for i, (dx, _) in enumerate(STEPS))
STEPS_Y = sum(dy * 4**i for i, (_, dy) in enumerate(STEPS))


def select(rows, cols, source):
    o = lax.broadcasted_iota(jnp.int32, (rows, cols), 0)
    i = lax.broadcasted_iota(jnp.int32, (rows, cols), 1)
    return jnp.where(source(o) == i, 1.0, 0.0).astype(BF16)


def select_back(rows, cols, source):
    i = lax.broadcasted_iota(jnp.int32, (rows, cols), 0)
    o = lax.broadcasted_iota(jnp.int32, (rows, cols), 1)
    return jnp.where(source(o) == i, 1.0, 0.0).astype(BF16)


def by_pair(s):
    return ((s >> 3) & 1) * 64 + (s >> 4) * 8 + (s & 7)


def by_stripe(o):
    return ((o >> 3) & 15) * 16 + ((o >> 2) & 1) * 8 + (o >> 7) * 4 + (o & 3)


def dot(a, b, ca=1, cb=0):
    return lax.dot_general(a, b, (((ca,), (cb,)), ((), ())), preferred_element_type=F32)


def unit(q, g, keys, values, low, high):
    scale = E ** (-0.5)
    s = dot(keys, q, 1, 1) * scale
    used = lax.broadcasted_iota(jnp.int32, (16, 128), 0) < S
    s = jnp.concatenate(
        [s[:128] + low, s[128:256], s[256:384] + high, jnp.where(used, s[384:], NEG)], axis=0
    )
    top = jnp.max(s, axis=0, keepdims=True)
    w = jnp.exp(s - top)
    p = w * (1.0 / jnp.sum(w, axis=0, keepdims=True))
    pb = p.astype(BF16)
    dprob = dot(values, g, 1, 1)
    delta = jnp.sum(pb.astype(F32) * dprob, axis=0, keepdims=True)
    ds = (p * ((dprob - delta) * scale)).astype(BF16)
    dk = dot(ds, q)
    dv = dot(pb, g)
    dq = dot(ds, keys, 0, 0)
    return dq, dk, dv


def kernel(
    qh_ref, kh_ref, vh_ref, gh_ref, slots_h_ref, decay_h_ref,
    oq_ref, ok_ref, ov_ref,
    q_ref, k_ref, v_ref, g_ref, slots_ref, decay_ref, wts,
    ms, rs, zp, zb, bp, bt, mp, mem, memk, memv,
    ms2, rs2, zp2, zb2, bp2, bt2, mp2, mem2,
    m2, dm,
    cskv, csq, csg, crkv, crq, crg, sep, hr, hc, gs, gr, own, cown, cgs, cgr,
    bsq, bsk, bsv, brq, brk, brv,
    send, recv, load,
):
    r = lax.axis_index("row")
    n = lax.axis_index("group")
    blk = n // 8
    idx = n % 8
    x = r // 4
    y = r % 4
    hh = y // 2
    yh = y % 2
    jp = x + yh * (7 - 2 * x)

    def holder(pair, part):
        high = pair // 4
        low = pair % 4
        return (low + high * (3 - 2 * low)) * 4 + part * 2 + high

    def in_row(d):
        return lax.rem(r + d, ROWS)

    def around(visit):
        def body(d, c):
            dx, dy = c
            visit(lax.rem(x + dx % 4, 4), lax.rem(y + dy % 4, 4))
            return dx // 4, dy // 4

        lax.fori_loop(0, len(STEPS), body, (jnp.int32(STEPS_X), jnp.int32(STEPS_Y)))

    def in_block(d):
        return blk * 8 + lax.rem(idx + d, 8)

    def in_blocks(d):
        return lax.rem(blk + d, 4) * 8 + idx

    barrier = pltpu.get_barrier_semaphore()

    def greet(axis, pick, count):
        def body(d, c):
            pl.semaphore_signal(barrier, inc=1, device_id={axis: pick(d)}, device_id_type=MESH)
            return c

        lax.fori_loop(1, count, body, 0)

    greet("row", in_row, ROWS)
    greet("group", in_block, 8)
    greet("group", in_blocks, 4)

    pairs = ((kh_ref, k_ref), (vh_ref, v_ref), (qh_ref, q_ref), (gh_ref, g_ref))

    def fetch(a, part):
        cols = (slice(None), pl.ds(part * HALF, HALF))
        return pltpu.make_async_copy(
            pairs[a][0].at[cols], pairs[a][1].at[cols], load.at[a * 2 + part]
        )

    for a in range(4):
        for part in (1, 0):
            fetch(a, part).start()

    fetch_slots = pltpu.make_async_copy(slots_h_ref, slots_ref, load.at[8])
    fetch_decay = pltpu.make_async_copy(decay_h_ref, decay_ref, load.at[9])
    fetch_slots.start()
    fetch_decay.start()

    def push(src, dst, k, device):
        pltpu.make_async_remote_copy(
            src_ref=src, dst_ref=dst, send_sem=send.at[k], recv_sem=recv.at[k],
            device_id=device, device_id_type=MESH,
        ).start()

    def arrived(shape_of, k):
        pltpu.make_async_copy(shape_of, shape_of, recv.at[k]).wait()

    def left(shape_of, k):
        pltpu.make_async_copy(shape_of, shape_of, send.at[k]).wait()

    def push_all(axis, pick, count, src, dst, k):
        def body(d, c):
            t = pick(d)
            push(src(t), dst, k, {axis: t})
            return c

        lax.fori_loop(1, count, body, 0)

    def push_row(src, dst, k):
        def visit(tx, ty):
            t = tx * 4 + ty
            push(src(t), dst, k, {"row": t})

        around(visit)

    to_pair = select(128, 128, by_pair)
    mine = pl.ds(pl.multiple_of(hh * PART, 128), PART)

    def arrange(refs, to):
        def body(h, c):
            ln = pl.ds(pl.multiple_of(h * 256, 256), 256)
            wide = pl.ds(pl.multiple_of(HALF + h * 256, 256), 256)
            for a, ref in enumerate(refs):
                to[:, a, :, ln] = dot(to_pair, ref[:, wide]).astype(BF16).reshape(8, 16, 256)
            return c

        lax.fori_loop(0, 5, body, 0)

    fetch_slots.wait()
    fetch_decay.wait()
    for part in range(2):
        for a in range(2):
            fetch(a, part).wait()
    slot_iota = lax.broadcasted_iota(jnp.int32, (S, 64), 0)
    member = [jnp.where(slots_ref[f] == slot_iota, 1.0, 0.0) for f in range(2)]
    member_b = [m.astype(BF16) for m in member]
    count = jnp.sum(member[0] + member[1], axis=1, keepdims=True)
    for a, ref in enumerate((k_ref, v_ref)):
        total = dot(member_b[0], ref[0:64, :]) + dot(member_b[1], ref[64:128, :])
        for s in range(S):
            ms[a * S + s, :, 0:FEATS] = total[s : s + 1]
            ms[a * S + s, :, FEATS:] = jnp.broadcast_to(count[s : s + 1], (1, 128))
    rs[r] = ms[r]

    pl.semaphore_wait(barrier, 15 + 7 + 3)
    push_row(lambda t: ms.at[t], rs.at[r], 0)

    def scatter(source, to, k):
        def visit(tx, ty):
            tjp = tx + (ty % 2) * (7 - 2 * tx)
            lanes = pl.ds(pl.multiple_of((ty // 2) * PART, 128), PART)
            push(source.at[tjp, :, :, lanes], to.at[r], k, {"row": tx * 4 + ty})

        around(visit)

    arrange((k_ref, v_ref), cskv)
    scatter(cskv, crkv, 4)
    crkv[r] = cskv[jp, :, :, mine]
    for a, ref, cut, to in ((2, q_ref, csq, crq), (3, g_ref, csg, crg)):
        fetch(a, 1).wait()
        arrange((ref,), cut)
        to[r] = cut[jp, :, :, mine]

    log_rate = jnp.log(
        jnp.concatenate([jnp.full((1, 128), decay_ref[h], F32) for h in range(20)], axis=1)
    )

    def power(e):
        return jnp.exp(log_rate * e.astype(F32))

    for j in range(8):
        wts[j] = jnp.where(j < idx, power(idx - 1 - j), 0.0)
        wts[8 + j] = jnp.exp(log_rate * float(7 - j))
        wts[20 + j] = jnp.where(j > idx, power(j - idx - 1), 0.0)
        wts[28 + j] = jnp.exp(log_rate * float(j))
    for j in range(4):
        wts[16 + j] = jnp.where(j < blk, power(8 * (blk - 1 - j) + idx), 0.0)
        wts[36 + j] = jnp.where(j > blk, power(8 * (j - blk - 1) + 7 - idx), 0.0)

    fetch(2, 0).wait()
    fetch(3, 0).wait()

    def to_the_block(piece, zp_, zb_, k):
        zp_[0] = piece
        zb_[idx] = piece
        push_all("group", in_block, 8, lambda t: zp_.at[0], zb_.at[idx], k)

    def to_the_blocks(zb_, bp_, bt_, k, first):
        arrived(zb_.at[pl.ds(0, 7)], k - 1)
        whole = jnp.sum(zb_[...] * wts[first + 8 : first + 16], axis=0)
        bp_[0] = whole
        bt_[blk] = whole
        push_all("group", in_blocks, 4, lambda t: bp_.at[0], bt_.at[blk], k)
        return jnp.sum(zb_[...] * wts[first : first + 8], axis=0)

    def to_the_row(inside, bt_, mp_, mem_, k, first, norm_):
        arrived(bt_.at[pl.ds(0, 3)], k - 1)
        inside = inside + jnp.sum(bt_[...] * wts[first + 16 : first + 20], axis=0)
        if norm_ is not None:
            inside = inside * norm_
        mp_[0] = inside
        mem_[r] = inside
        push_row(lambda t: mp_.at[0], mem_.at[r], k)

    arrived(rs.at[pl.ds(0, 15)], 0)
    total = jnp.sum(rs[...], axis=0)
    norm = 1.0 / jnp.sqrt(jnp.maximum(total[:, FEATS : FEATS + 1], 1.0))
    to_the_block(total[:, :FEATS] * norm, zp, zb, 1)
    scatter(csq, crq, 21)

    to_stripe = select(256, 256, by_stripe)

    def split(from_, a, to):
        block = from_[:, a, :, :].reshape(256, PART)
        sep[to] = dot(to_stripe, block).astype(BF16).reshape(2, 128, PART)

    pair_before = holder(lax.rem(jp + 7, 8), hh)
    pair_after = holder(lax.rem(jp + 1, 8), hh)
    arrived(crkv.at[pl.ds(0, 15)], 4)
    split(crkv, 0, 1)
    split(crkv, 1, 2)
    inside = to_the_blocks(zb, bp, bt, 2, 0)
    push(sep.at[pl.ds(1, 2), 0], hc.at[1], 9, {"row": pair_before})
    push(sep.at[pl.ds(1, 2), 1], hc.at[0], 10, {"row": pair_after})
    scatter(csg, crg, 12)
    to_the_row(inside, bt, mp, mem, 3, 0, None)

    before = lax.rem(r + ROWS - 1, ROWS)
    after = lax.rem(r + 1, ROWS)
    for i in range(2):
        cols = (slice(None), pl.ds(i * PART, PART))
        for a, ref in enumerate((k_ref, v_ref)):
            push(ref.at[cols], hr.at[i, 1, a], 22 + 4 * i + 2 * a, {"row": before})
            push(ref.at[cols], hr.at[i, 0, a], 23 + 4 * i + 2 * a, {"row": after})
    arrived(crq.at[pl.ds(0, 15)], 21)
    split(crq, 0, 0)
    arrived(crg.at[pl.ds(0, 15)], 12)
    split(crg, 0, 3)

    arrived(mem.at[pl.ds(0, 15)], 3)
    zero = jnp.zeros((S, FEATS), F32)
    m2[S:, :] = zero
    for a, to in enumerate((memk, memv)):
        for s in range(S):
            m2[s : s + 1, :] = mem[a * S + s]
        to[...] = m2[...].astype(BF16)
    dm[0] = zero
    dm[1] = zero

    arrived(hc.at[1], 9)
    arrived(hc.at[0], 10)
    col_low = jnp.where(jp > 0, 0.0, NEG)
    col_high = jnp.where(jp < 7, 0.0, NEG)

    def col_head(h, c):
        ln = pl.ds(pl.multiple_of(h * E, E), E)
        wide = pl.ds(pl.multiple_of(HALF + hh * PART + h * E, E), E)
        mk = memk[:, wide]
        mv = memv[:, wide]
        k0, k1, k2, k3 = hc[0, 0, :, ln], sep[1, 0, :, ln], sep[1, 1, :, ln], hc[1, 0, :, ln]
        v0, v1, v2, v3 = hc[0, 1, :, ln], sep[2, 0, :, ln], sep[2, 1, :, ln], hc[1, 1, :, ln]
        qa, ka, va = unit(
            sep[0, 0, :, ln], sep[3, 0, :, ln],
            jnp.concatenate([k0, k1, k2, mk], axis=0), jnp.concatenate([v0, v1, v2, mv], axis=0),
            col_low, 0.0,
        )
        qb, kb, vb = unit(
            sep[0, 1, :, ln], sep[3, 1, :, ln],
            jnp.concatenate([k1, k2, k3, mk], axis=0), jnp.concatenate([v1, v2, v3, mv], axis=0),
            0.0, col_high,
        )
        for a, (da, db) in enumerate(((ka, kb), (va, vb))):
            cgs[0, a, :, ln] = da[0:128].astype(BF16)
            cown[a, :, ln] = da[128:384] + db[0:256]
            cgs[1, a, :, ln] = db[256:384].astype(BF16)
            dm[a, :, wide] = da[384:392] + db[384:392]
        sep[0, 0, :, ln] = qa.astype(BF16)
        sep[0, 1, :, ln] = qb.astype(BF16)
        return c

    lax.fori_loop(0, 5, col_head, 0, unroll=True)
    push(cgs.at[0], cgr.at[1], 13, {"row": pair_before})
    push(cgs.at[1], cgr.at[0], 14, {"row": pair_after})
    from_stripe = select_back(256, 256, by_stripe)
    bsq[...] = dot(from_stripe, sep[0].reshape(256, PART)).astype(BF16).reshape(16, 16, PART)
    brq[jp, :, mine] = bsq[r]

    row_low = jnp.where(r > 0, 0.0, NEG)
    row_high = jnp.where(r < ROWS - 1, 0.0, NEG)

    def row_heads(i):
        for k in range(4):
            arrived(hr.at[0, 0, 0], 22 + 4 * i + k)

        def body(h, c):
            near = pl.ds(pl.multiple_of(h * E, E), E)
            ln = pl.ds(pl.multiple_of(i * PART + h * E, E), E)
            keys = jnp.concatenate(
                [hr[i, 0, 0, :, near], k_ref[:, ln], hr[i, 1, 0, :, near], memk[:, ln]], axis=0
            )
            vals = jnp.concatenate(
                [hr[i, 0, 1, :, near], v_ref[:, ln], hr[i, 1, 1, :, near], memv[:, ln]], axis=0
            )
            dq, dk, dv = unit(q_ref[:, ln], g_ref[:, ln], keys, vals, row_low, row_high)
            oq_ref[:, ln] = dq.astype(BF16)
            for a, d in enumerate((dk, dv)):
                gs[i, 0, a, :, near] = d[0:128].astype(BF16)
                own[a, :, ln] = d[128:256]
                gs[i, 1, a, :, near] = d[256:384].astype(BF16)
                dm[a, :, ln] = d[384:392]
            return c

        lax.fori_loop(0, 5, body, 0, unroll=True)

    def row_back(i):
        push(gs.at[i, 0], gr.at[i, 1], 5 + 2 * i, {"row": before})
        push(gs.at[i, 1], gr.at[i, 0], 6 + 2 * i, {"row": after})

    row_heads(0)
    row_heads(1)

    for a in range(2):
        for s in range(S):
            ms2[a * S + s] = dm[a, s : s + 1, :]
    rs2[r] = ms2[r]
    push_row(lambda t: ms2.at[t], rs2.at[r], 15)
    row_back(0)
    push_row(lambda t: bsq.at[t], brq.at[jp, :, mine], 19)

    arrived(cgr.at[1], 13)
    arrived(cgr.at[0], 14)
    for a, (cut, to) in enumerate(((bsk, brk), (bsv, brv))):
        full = jnp.concatenate(
            [
                cown[a, 0:128, :] + cgr[0, a].astype(F32),
                cown[a, 128:256, :] + cgr[1, a].astype(F32),
            ],
            axis=0,
        ).astype(BF16)
        cut[...] = dot(from_stripe, full).astype(BF16).reshape(16, 16, PART)
        to[jp, :, mine] = cut[r]

    arrived(rs2.at[pl.ds(0, 15)], 15)
    to_the_block(jnp.sum(rs2[...], axis=0), zp2, zb2, 16)
    push_row(lambda t: bsk.at[t], brk.at[jp, :, mine], 20)
    inside = to_the_blocks(zb2, bp2, bt2, 17, 20)
    push_row(lambda t: bsv.at[t], brv.at[jp, :, mine], 11)
    to_the_row(inside, bt2, mp2, mem2, 18, 20, norm)
    row_back(1)

    from_pair = select_back(128, 128, by_pair)
    arrived(bsq.at[pl.ds(0, 15)], 19)

    def finish_q(h, c):
        ln = pl.ds(pl.multiple_of(h * 256, 256), 256)
        wide = pl.ds(pl.multiple_of(HALF + h * 256, 256), 256)
        oq_ref[:, wide] = dot(from_pair, brq[:, :, ln].reshape(128, 256)).astype(BF16)
        return c

    lax.fori_loop(0, 5, finish_q, 0)
    for i in range(2):
        cols = pl.ds(i * PART, PART)
        arrived(gr.at[i, 0], 5 + 2 * i)
        arrived(gr.at[i, 1], 6 + 2 * i)
        for a in range(2):
            own[a, :, cols] = (
                own[a, :, cols] + gr[i, 0, a].astype(F32) + gr[i, 1, a].astype(F32)
            )
    arrived(mem2.at[pl.ds(0, 15)], 18)
    for a in range(2):
        for s in range(S):
            dm[a, s : s + 1, :] = mem2[a * S + s]
    arrived(bsk.at[pl.ds(0, 15)], 20)
    arrived(bsv.at[pl.ds(0, 15)], 11)

    def finish(h, c):
        ln = pl.ds(pl.multiple_of(h * 256, 256), 256)
        wide = pl.ds(pl.multiple_of(HALF + h * 256, 256), 256)
        for a, (from_, out) in enumerate(((brk, ok_ref), (brv, ov_ref))):
            back = dot(from_pair, from_[:, :, ln].reshape(128, 256))
            dr = dm[a, :, ln].astype(BF16)
            dc = dm[a, :, wide].astype(BF16)
            add_r = jnp.concatenate([dot(member_b[f], dr, 0, 0) for f in range(2)], axis=0)
            add_c = jnp.concatenate([dot(member_b[f], dc, 0, 0) for f in range(2)], axis=0)
            out[:, ln] = (own[a, :, ln] + add_r).astype(BF16)
            out[:, wide] = (back + add_c).astype(BF16)
        return c

    lax.fori_loop(0, 5, finish, 0)

    left(ms.at[pl.ds(0, 15)], 0)
    left(zb.at[pl.ds(0, 7)], 1)
    left(bt.at[pl.ds(0, 3)], 2)
    left(mem.at[pl.ds(0, 15)], 3)
    left(crkv.at[pl.ds(0, 15)], 4)
    left(crq.at[pl.ds(0, 15)], 21)
    left(crg.at[pl.ds(0, 15)], 12)
    for k in range(8):
        left(hr.at[0, 0, 0], 22 + k)
    for k in range(4):
        left(gs.at[0, 0], 5 + k)
    left(hc.at[1], 9)
    left(hc.at[0], 10)
    left(cgs.at[0], 13)
    left(cgs.at[1], 14)
    left(ms2.at[pl.ds(0, 15)], 15)
    left(zb2.at[pl.ds(0, 7)], 16)
    left(bt2.at[pl.ds(0, 3)], 17)
    left(mem2.at[pl.ds(0, 15)], 18)
    left(bsq.at[pl.ds(0, 15)], 19)
    left(bsk.at[pl.ds(0, 15)], 20)
    left(bsv.at[pl.ds(0, 15)], 11)


def per_device(queries, keys, values, out_grad, slots, decay):
    flat = (TOKENS, FEATS)
    vm = pl.BlockSpec(memory_space=pltpu.VMEM)

    def row(count, width=FEATS):
        return pltpu.VMEM((count, 1, width), F32)

    scratch = [
        *[pltpu.VMEM(flat, BF16)] * 4,
        pltpu.VMEM(slots.shape, jnp.int32), pltpu.SMEM(decay.shape, F32), row(40),
        row(16, FEATS + 128), row(16, FEATS + 128),
        row(1), row(8), row(1), row(4), row(1), row(16),
        pltpu.VMEM((16, FEATS), BF16), pltpu.VMEM((16, FEATS), BF16),
        row(16), row(16),
        row(1), row(8), row(1), row(4), row(1), row(16),
        pltpu.VMEM((16, FEATS), F32), pltpu.VMEM((2, S, FEATS), F32),
        pltpu.VMEM((8, 2, 16, HALF), BF16),
        pltpu.VMEM((8, 1, 16, HALF), BF16),
        pltpu.VMEM((8, 1, 16, HALF), BF16),
        pltpu.VMEM((16, 2, 16, PART), BF16),
        pltpu.VMEM((16, 1, 16, PART), BF16),
        pltpu.VMEM((16, 1, 16, PART), BF16),
        pltpu.VMEM((4, 2, 128, PART), BF16),
        pltpu.VMEM((2, 2, 2, 128, PART), BF16),
        pltpu.VMEM((2, 2, 128, PART), BF16),
        pltpu.VMEM((2, 2, 2, 128, PART), BF16),
        pltpu.VMEM((2, 2, 2, 128, PART), BF16),
        pltpu.VMEM((2, 128, HALF), F32),
        pltpu.VMEM((2, 256, PART), F32),
        pltpu.VMEM((2, 2, 128, PART), BF16),
        pltpu.VMEM((2, 2, 128, PART), BF16),
        *[pltpu.VMEM((16, 16, PART), BF16)] * 3,
        *[pltpu.VMEM((8, 16, HALF), BF16)] * 3,
        pltpu.SemaphoreType.DMA((30,)),
        pltpu.SemaphoreType.DMA((30,)),
        pltpu.SemaphoreType.DMA((10,)),
    ]
    outs = pl.pallas_call(
        kernel,
        out_shape=[jax.ShapeDtypeStruct(flat, BF16)] * 3,
        in_specs=[pl.BlockSpec(memory_space=pltpu.HBM)] * 6,
        out_specs=[vm] * 3,
        scratch_shapes=scratch,
        compiler_params=pltpu.CompilerParams(
            collective_id=0, has_side_effects=True, vmem_limit_bytes=48 * 1024 * 1024
        ),
    )(
        *[
            pltpu.with_memory_space_constraint(a, pltpu.HBM)
            for a in (
                queries.reshape(flat), keys.reshape(flat), values.reshape(flat),
                out_grad.reshape(flat), slots, decay,
            )
        ],
    )
    return tuple(o.reshape(queries.shape) for o in outs)


def solution(mesh):
    spec = P("group", "row", None, None)
    return jax.shard_map(
        per_device,
        mesh=mesh,
        in_specs=(spec, spec, spec, spec, P("group", "row", None), P()),
        out_specs=(spec, spec, spec),
        check_vma=False,
    )
```
